512 devices in a mesh: dp: 32 (over x, y, core), seq: 16 (over z).
Axes of the slice: x: 4, y: 4, z: 16, core: 2. Of those that a mesh axis runs over, the one named last changes fastest.
Arguments:
- queries: bfloat16 [262144, 1152], P(('dp', 'seq')), parts along dimension 0, may hold values from -8 to 8
- key_rows: bfloat16 [262144, 1152], P(('dp', 'seq')), parts along dimension 0, may hold values from -8 to 8
- value_rows: bfloat16 [262144, 1152], P(('dp', 'seq')), parts along dimension 0, may hold values from -6 to 6
- offset_two: int32 [18], replicated, may hold values from 0 to 1
- offset_four: int32 [18], replicated, may hold values from 0 to 3
- offset_pair: int32 [18], replicated, may hold values from 0 to 7
- offset_far: int32 [18], replicated, may hold values from 0 to 63
Outputs:
- attended: bfloat16 [262144, 1152], P(('dp', 'seq')), parts along dimension 0
The draws below stay inside these ranges and needn't reach their ends.
There are 32 independent parts, one for each index of `dp`. The reference program is written for one: setup_inputs(seed, part) draws one part's arguments, and reference() takes and returns one part's arrays. A program takes and returns all parts, laid end to end along the dimension named above; an argument that names none is the same for every part. Nothing has to cross between parts.
All inputs are finite; a program needn't handle non-finite values.
Results may differ from the reference program's by a relative error of at most 0.0032.
Values may be sent and summed in bfloat16 or wider, within the bound.
A program may use at most 64 MiB of HBM per device.

```python
import jax
import jax.numpy as jnp
from jax import lax

HEADS = 18
HEAD_DIM = 64
TOK_DEV = 512
R_TWO = 2
R_FOUR = 4
R_PAIR = 8
R_FAR = 64
TOKENS = 8192


def draw_queries(key, part):
    key = jax.random.fold_in(key, 11)
    second = jax.random.fold_in(key, 1)
    noise = jax.random.normal(second, (TOKENS, HEADS * HEAD_DIM), jnp.float32)
    return jnp.clip(1.4 * noise, -8.0, 8.0).astype(jnp.bfloat16)


def draw_key_rows(key, part):
    key = jax.random.fold_in(key, 12)
    second = jax.random.fold_in(key, 1)
    noise = jax.random.normal(second, (TOKENS, HEADS * HEAD_DIM), jnp.float32)
    return jnp.clip(1.4 * noise, -8.0, 8.0).astype(jnp.bfloat16)


def plant(drawn, own_key, low, largest):
    extent = drawn.shape
    index_at = [jax.random.randint(jax.random.fold_in(own_key, axis), (), 0, extent[axis]) for axis in range(len(extent))]
    drawn = drawn.at[tuple(index_at)].set(low)
    longest = extent.index(max(extent))
    index_at[longest] = (index_at[longest] + 1) % extent[longest]
    return drawn.at[tuple(index_at)].set(largest)


def block_scale(key, extent, cuts, low, high):
    def one(position, parts):
        heights = jax.random.uniform(jax.random.fold_in(jax.random.fold_in(key, 6), position), (parts,), jnp.float32, low / len(cuts), high / len(cuts))
        return jnp.repeat(jnp.exp(heights), extent[position] // parts).reshape((-1,) + (1,) * (len(extent) - position - 1))

    level = one(*cuts[0])
    for cut in cuts[1:]:
        level = level * one(*cut)
    return level


def gaussian(key, dims, deviation, most, cuts=(), kind=jnp.bfloat16):
    gain = block_scale(key, dims, cuts, -0.22, 0.18) if cuts else 1.0
    values = jax.random.normal(key, dims, jnp.float32) * deviation * gain
    return jnp.minimum(jnp.maximum(values, -most), most).astype(kind)


def setup_inputs(seed: int = 0, part: int = 0) -> dict:
    key_of = jax.random.split(jax.random.key(seed), 8)
    part_splits = jax.random.split(jax.random.fold_in(key_of[7], part), 8)
    return {
        "queries": draw_queries(jax.random.fold_in(jax.random.fold_in(key_of[7], part), 71), part),
        "key_rows": draw_key_rows(jax.random.fold_in(jax.random.fold_in(key_of[7], part), 71), part),
        "value_rows": gaussian(part_splits[2], (TOKENS, HEADS * HEAD_DIM), 1.0, 6.0, ((0, 16),)),
        "offset_two": plant(jax.random.randint(key_of[3], (HEADS,), 0, R_TWO), jax.random.fold_in(key_of[3], 1), 0, R_TWO - 1).astype(jnp.int32),
        "offset_four": plant(jax.random.randint(key_of[4], (HEADS,), 0, R_FOUR), jax.random.fold_in(key_of[4], 1), 0, R_FOUR - 1).astype(jnp.int32),
        "offset_pair": plant(jax.random.randint(key_of[5], (HEADS,), 0, R_PAIR), jax.random.fold_in(key_of[5], 1), 0, R_PAIR - 1).astype(jnp.int32),
        "offset_far": plant(jax.random.randint(key_of[6], (HEADS,), 0, R_FAR), jax.random.fold_in(key_of[6], 1), 0, R_FAR - 1).astype(jnp.int32),
    }


def head_mask(dilation, offsets, head_size):
    phases = lax.broadcasted_iota(jnp.int32, (dilation, offsets.shape[0] * head_size), 0)
    return phases == jnp.repeat(offsets, head_size)[None, :]


def select(source, dilation, offsets, head_size):
    row_count, row_width = source.shape
    shaped = source.reshape(row_count // dilation, dilation, row_width)
    selector = head_mask(dilation, offsets, head_size)
    return jnp.sum(jnp.where(selector[None], shaped, jnp.zeros((), source.dtype)), axis=1).astype(source.dtype)


def spread(result, log_total, dilation, offsets, head_size):
    row_count, row_width = result.shape
    head_count = offsets.shape[0]
    selector = head_mask(dilation, offsets, head_size)
    expanded = jnp.where(selector[None], result[:, None, :], jnp.zeros((), result.dtype)).reshape(row_count * dilation, row_width)
    phases = lax.broadcasted_iota(jnp.int32, (dilation, head_count), 0)
    covered = phases == offsets[None, :]
    log_totals = jnp.where(covered[None], log_total[:, None, :], jnp.zeros((), log_total.dtype)).reshape(row_count * dilation, head_count)
    covered_full = jnp.broadcast_to(covered[None], (row_count, dilation, head_count)).reshape(row_count * dilation, head_count)
    return expanded, log_totals, covered_full


def attend(query_block, key_block, value_block, head_size):
    row_count, row_width = query_block.shape
    head_count = row_width // head_size
    shaped_query = query_block.reshape(row_count, head_count, head_size).astype(jnp.float32)
    shaped_key = key_block.reshape(key_block.shape[0], head_count, head_size).astype(jnp.float32)
    shaped_value = value_block.reshape(value_block.shape[0], head_count, head_size).astype(jnp.float32)
    scores = jnp.einsum("qhd,khd->hqk", shaped_query, shaped_key) * (head_size ** -0.5)
    highest = jnp.max(scores, axis=2, keepdims=True)
    raised = jnp.exp(scores - highest)
    totals = jnp.sum(raised, axis=2)
    weights = lax.optimization_barrier(raised.astype(jnp.bfloat16)).astype(jnp.float32)
    summed = jnp.einsum("hqk,khd->qhd", weights, shaped_value)
    result = summed / totals.T[:, :, None]
    log_total = (highest[:, :, 0] + jnp.log(totals)).T
    return result.reshape(row_count, row_width), log_total


def branch(queries, key_rows, value_rows, segment, dilation, offsets, head_size):
    row_width = queries.shape[1]
    head_count = offsets.shape[0]

    def one_segment(segment_index):
        first_row = segment_index * segment
        picked = [select(lax.dynamic_slice_in_dim(source, first_row, segment, 0), dilation, offsets, head_size) for source in (queries, key_rows, value_rows)]
        result, log_total = attend(picked[0], picked[1], picked[2], head_size)
        return spread(result, log_total, dilation, offsets, head_size)

    expanded, log_totals, covered = lax.map(one_segment, jnp.arange(queries.shape[0] // segment, dtype=jnp.int32))
    return expanded.reshape(-1, row_width), log_totals.reshape(-1, head_count), covered.reshape(-1, head_count)


def combine(branches, head_size):
    row_count, row_width = branches[0][0].shape
    head_count = row_width // head_size
    highest = branches[0][1]
    for result, log_totals, covered in branches[1:]:
        highest = jnp.maximum(highest, jnp.where(covered, log_totals, highest))
    numerator = jnp.zeros((row_count, head_count, head_size), jnp.float32)
    denominator = jnp.zeros((row_count, head_count), jnp.float32)
    for result, log_totals, covered in branches:
        factor = jnp.where(covered, jnp.exp(log_totals - highest), jnp.zeros((), jnp.float32))
        numerator = numerator + factor[:, :, None] * result.reshape(row_count, head_count, head_size)
        denominator = denominator + factor
    return (numerator / denominator[:, :, None]).reshape(row_count, row_width).astype(jnp.bfloat16)


def reference(queries, key_rows, value_rows, offset_two, offset_four, offset_pair, offset_far):
    head_size = HEAD_DIM
    zero_offsets = jnp.zeros((HEADS,), jnp.int32)
    branches = [
        branch(queries, key_rows, value_rows, TOK_DEV, 1, zero_offsets, head_size),
        branch(queries, key_rows, value_rows, TOK_DEV, R_TWO, offset_two, head_size),
        branch(queries, key_rows, value_rows, TOK_DEV, R_FOUR, offset_four, head_size),
        branch(queries, key_rows, value_rows, 2 * TOK_DEV, R_PAIR, offset_pair, head_size),
        branch(queries, key_rows, value_rows, TOKENS, R_FAR, offset_far, head_size),
    ]
    return combine(branches, head_size)
```

```python
import functools
import math

import jax
import jax.numpy as jnp
from jax import lax
from jax.experimental import pallas as pl
from jax.experimental.pallas import tpu as pltpu
from jax.sharding import PartitionSpec as P

R_TWO = 2
R_FOUR = 4
R_PAIR = 8
R_FAR = 64

ROWS = 512
HEADS = 18
HEAD = 64
WIDTH = HEADS * HEAD
GROUPS = HEADS // 2
LANES = 128
SHARDS = 16
PAIR_ROWS = ROWS // R_PAIR
FAR_ROWS = ROWS // R_FAR
SCALE = HEAD**-0.5 * math.log2(math.e)
LOW = -1e30

F32 = jnp.float32
BF16 = jnp.bfloat16


def iota(shape, dimension):
    return lax.broadcasted_iota(jnp.int32, shape, dimension)


def dot_t(a, b):
    return lax.dot_general(a, b, (((1,), (1,)), ((), ())), preferred_element_type=F32)


def dot(a, b):
    return lax.dot_general(a, b, (((1,), (0,)), ((), ())), preferred_element_type=F32)


def lane_offsets(ref, group, shape):
    first = iota(shape, len(shape) - 1) < HEAD
    return jnp.where(first, ref[2 * group], ref[2 * group + 1])


def kernel(
    off_two, off_four, off_pair, off_far, q_ref, k_ref, v_ref, out_ref,
    pair_send, pair_recv, far, q_pair, q_far, num, tot, top,
    pair_sems, right_send, right_recv, left_send, left_recv,
):
    me = lax.axis_index("seq")
    right = lax.rem(me + 1, SHARDS)
    left = lax.rem(me + SHARDS - 1, SHARDS)
    partner = me + 1 - 2 * lax.rem(me, 2)

    barrier = pltpu.get_barrier_semaphore()
    for neighbour in (left, right):
        pl.semaphore_signal(barrier, inc=1, device_id={"seq": neighbour})

    def columns(group):
        return pl.ds(pl.multiple_of(group * LANES, LANES), LANES)

    pair_copy = pltpu.make_async_remote_copy(
        src_ref=pair_send,
        dst_ref=pair_recv,
        send_sem=pair_sems.at[0],
        recv_sem=pair_sems.at[1],
        device_id={"seq": partner},
    )

    def right_copy(step):
        slot = lax.rem(me - step + SHARDS, SHARDS)
        return pltpu.make_async_remote_copy(
            src_ref=far.at[slot],
            dst_ref=far.at[slot],
            send_sem=right_send.at[step],
            recv_sem=right_recv.at[step],
            device_id={"seq": right},
        )

    def left_copy(step):
        slot = lax.rem(me + step, SHARDS)
        return pltpu.make_async_remote_copy(
            src_ref=far.at[slot],
            dst_ref=far.at[slot],
            send_sem=left_send.at[step],
            recv_sem=left_recv.at[step],
            device_id={"seq": left},
        )

    gather_pair = (iota((PAIR_ROWS, ROWS), 1) // R_PAIR == iota((PAIR_ROWS, ROWS), 0)).astype(F32).astype(BF16)
    gather_far = (iota((16, LANES), 1) // 16 == lax.rem(iota((16, LANES), 0), FAR_ROWS)).astype(F32).astype(BF16)

    def pick_far(source, group):
        shaped = source[:, columns(group)].reshape(FAR_ROWS, R_FAR // 16, 16, LANES)
        offsets = lane_offsets(off_far, group, (R_FAR // 16, 16, LANES))
        rows = iota((R_FAR // 16, 16, LANES), 0) * 16 + iota((R_FAR // 16, 16, LANES), 1)
        mask = (rows == offsets).astype(F32).astype(BF16)
        picked = jnp.sum(shaped * mask[None], axis=1).reshape(FAR_ROWS * 16, LANES)
        return dot(gather_far, picked.astype(BF16)).astype(BF16)

    def pick_pair(source, group):
        shaped = source[:, columns(group)].reshape(ROWS // 16, 16, LANES)
        offsets = lane_offsets(off_pair, group, (16, LANES))
        mask = (lax.rem(iota((16, LANES), 0), R_PAIR) == offsets).astype(F32).astype(BF16)
        picked = (shaped * mask[None]).reshape(ROWS, LANES)
        return dot(gather_pair, picked).astype(BF16)

    def select_far(group, carry):
        keys = pick_far(k_ref, group)
        values = pick_far(v_ref, group)
        low = iota((16, LANES), 0) < FAR_ROWS
        far[me, :, columns(group)] = jnp.where(low, keys.astype(F32), values.astype(F32)).astype(BF16)
        return carry

    def select_pair(group, carry):
        pair_send[0:PAIR_ROWS, columns(group)] = pick_pair(k_ref, group)
        pair_send[PAIR_ROWS:, columns(group)] = pick_pair(v_ref, group)
        return carry

    def select_queries(group, carry):
        q_pair[:, columns(group)] = pick_pair(q_ref, group)
        q_far[:, columns(group)] = pick_far(q_ref, group)
        return carry

    lax.fori_loop(0, GROUPS, select_far, 0)
    pl.semaphore_wait(barrier, 2)
    right_copy(0).start()
    left_copy(0).start()
    lax.fori_loop(0, GROUPS, select_pair, 0)
    pair_copy.start()
    lax.fori_loop(0, GROUPS, select_queries, 0)

    first_lanes = iota((1, LANES), 1) < HEAD
    head_lanes = [
        first_lanes.astype(F32).astype(BF16),
        (~first_lanes).astype(F32).astype(BF16),
    ]

    def dense(group, carry):
        @pl.when(jnp.logical_and(group >= 1, group <= 8))
        def _():
            right_copy(group - 1).wait()

        @pl.when(jnp.logical_and(group >= 1, group <= 7))
        def _():
            left_copy(group - 1).wait()
            right_copy(group).start()

        @pl.when(jnp.logical_and(group >= 1, group <= 6))
        def _():
            left_copy(group).start()

        queries = q_ref[:, columns(group)]
        keys = k_ref[:, columns(group)]
        values = jnp.concatenate([v_ref[:, columns(group)], jnp.ones((ROWS, LANES), BF16)], axis=1)
        results, tops = [], []
        for parity in range(2):
            two = off_two[2 * group + parity]
            four = off_four[2 * group + parity]
            rows, cols = iota((8, LANES), 0), iota((8, LANES), 1)
            in_two = jnp.logical_and(rows % R_TWO == two, cols % R_TWO == two)
            in_four = jnp.logical_and(rows % R_FOUR == four, cols % R_FOUR == four)
            times = 1.0 + in_two.astype(F32) + in_four.astype(F32)
            times = jnp.concatenate([times] * (ROWS // LANES), axis=1)
            scores = dot_t(queries * head_lanes[parity], keys)
            highest = jnp.max(scores, axis=1, keepdims=True)
            raised = jnp.exp2((scores - highest) * SCALE)
            weights = (raised.reshape(ROWS // 8, 8, ROWS) * times[None]).reshape(ROWS, ROWS)
            results.append(dot(weights.astype(BF16), values))
            tops.append(highest)
        num[:, columns(group)] = jnp.where(first_lanes, results[0][:, :LANES], results[1][:, :LANES])
        tot[:, columns(group)] = jnp.where(first_lanes, results[0][:, LANES:], results[1][:, LANES:])
        top[:, columns(group)] = jnp.where(first_lanes, tops[0], tops[1])
        return carry

    lax.fori_loop(0, GROUPS, dense, 0)
    pair_copy.wait()

    def finish(group, carry):
        cols = columns(group)
        queries = q_pair[:, cols]
        queries = jnp.concatenate([queries * head_lanes[0], queries * head_lanes[1]], axis=0)
        keys = jnp.concatenate([pair_send[0:PAIR_ROWS, cols], pair_recv[0:PAIR_ROWS, cols]], axis=0)
        values = jnp.concatenate([pair_send[PAIR_ROWS:, cols], pair_recv[PAIR_ROWS:, cols]], axis=0)
        values = jnp.concatenate([values, jnp.ones((2 * PAIR_ROWS, LANES), BF16)], axis=1)
        scores = dot_t(queries, keys)
        highest = jnp.max(scores, axis=1, keepdims=True)
        weights = jnp.exp2((scores - highest) * SCALE).astype(BF16)
        result = dot(weights, values)
        pair_num = jnp.where(first_lanes, result[:PAIR_ROWS, :LANES], result[PAIR_ROWS:, :LANES])
        pair_tot = jnp.where(first_lanes, result[:PAIR_ROWS, LANES:], result[PAIR_ROWS:, LANES:])
        pair_top = jnp.where(first_lanes, highest[:PAIR_ROWS], highest[PAIR_ROWS:])

        queries = q_far[:, cols]
        low = iota((16, LANES), 0) < FAR_ROWS
        keep = low == (iota((16, LANES), 1) < HEAD)
        queries = jnp.where(keep, queries.astype(F32), 0.0).astype(BF16)
        rows = far[:, :, cols].reshape(SHARDS * 16, LANES)
        scores = dot_t(queries, rows)
        is_key = lax.rem(iota((16, SHARDS * 16), 1), 16) < FAR_ROWS
        scores = jnp.where(is_key, scores, LOW)
        highest = jnp.max(scores, axis=1, keepdims=True)
        weights = pltpu.roll(jnp.exp2((scores - highest) * SCALE), FAR_ROWS, 1).astype(BF16)
        rows = jnp.concatenate([rows, jnp.ones((SHARDS * 16, LANES), BF16)], axis=1)
        result = dot(weights, rows)
        far_num = jnp.where(first_lanes, result[:FAR_ROWS, :LANES], result[FAR_ROWS:, :LANES])
        far_tot = jnp.where(first_lanes, result[:FAR_ROWS, LANES:], result[FAR_ROWS:, LANES:])
        far_top = jnp.where(first_lanes, highest[:FAR_ROWS], highest[FAR_ROWS:])

        shape = (FAR_ROWS, R_FAR // R_PAIR, 8, LANES)
        own_num = num[:, cols].reshape(shape)
        own_tot = tot[:, cols].reshape(shape)
        own_top = top[:, cols].reshape(shape)
        pair_num, pair_tot, pair_top = (
            jnp.broadcast_to(each.reshape(PAIR_ROWS, 1, LANES), (PAIR_ROWS, 8, LANES)).reshape(shape)
            for each in (pair_num, pair_tot, pair_top)
        )
        far_num, far_tot, far_top = (
            jnp.broadcast_to(each.reshape(FAR_ROWS, 1, LANES), (FAR_ROWS, 8, LANES)).reshape(FAR_ROWS, 1, 8, LANES)
            for each in (far_num, far_tot, far_top)
        )
        phase = iota((8, LANES), 0)
        pair_in = phase == lane_offsets(off_pair, group, (8, LANES))
        far_phase = iota((R_FAR // 8, 8, LANES), 0) * 8 + iota((R_FAR // 8, 8, LANES), 1)
        far_in = far_phase == lane_offsets(off_far, group, (R_FAR // 8, 8, LANES))
        pair_top = jnp.where(pair_in[None, None], pair_top, LOW)
        far_top = jnp.where(far_in[None], far_top, LOW)
        peak = jnp.maximum(own_top, jnp.maximum(pair_top, far_top))
        own_factor = jnp.exp2((own_top - peak) * SCALE)
        pair_factor = jnp.exp2((pair_top - peak) * SCALE)
        far_factor = jnp.exp2((far_top - peak) * SCALE)
        upper = own_factor * own_num + pair_factor * pair_num + far_factor * far_num
        lower = own_factor * own_tot + pair_factor * pair_tot + far_factor * far_tot
        out_ref[:, cols] = (upper / lower).reshape(ROWS, LANES).astype(BF16)
        return carry

    lax.fori_loop(0, GROUPS, finish, 0)


def local(queries, key_rows, value_rows, offset_two, offset_four, offset_pair, offset_far):
    vmem = pl.BlockSpec(memory_space=pltpu.VMEM)
    smem = pl.BlockSpec(memory_space=pltpu.SMEM)
    return pl.pallas_call(
        kernel,
        out_shape=jax.ShapeDtypeStruct((ROWS, WIDTH), BF16),
        in_specs=[smem] * 4 + [vmem] * 3,
        out_specs=vmem,
        scratch_shapes=[
            pltpu.VMEM((2 * PAIR_ROWS, WIDTH), BF16),
            pltpu.VMEM((2 * PAIR_ROWS, WIDTH), BF16),
            pltpu.VMEM((SHARDS, 16, WIDTH), BF16),
            pltpu.VMEM((PAIR_ROWS, WIDTH), BF16),
            pltpu.VMEM((16, WIDTH), BF16),
            pltpu.VMEM((ROWS, WIDTH), F32),
            pltpu.VMEM((ROWS, WIDTH), F32),
            pltpu.VMEM((ROWS, WIDTH), F32),
            pltpu.SemaphoreType.DMA((2,)),
            pltpu.SemaphoreType.DMA((8,)),
            pltpu.SemaphoreType.DMA((8,)),
            pltpu.SemaphoreType.DMA((8,)),
            pltpu.SemaphoreType.DMA((8,)),
        ],
        compiler_params=pltpu.CompilerParams(
            collective_id=0, has_side_effects=True, vmem_limit_bytes=48 * 1024 * 1024
        ),
        cost_estimate=pl.CostEstimate(flops=2 * 10**9, bytes_accessed=5 * 10**6, transcendentals=6 * 10**6),
        name="dilated_attention",
    )(offset_two, offset_four, offset_pair, offset_far, queries, key_rows, value_rows)


def solution(mesh):
    rows = P(("dp", "seq"), None)
    return jax.shard_map(
        local, mesh=mesh, in_specs=(rows,) * 3 + (P(),) * 4, out_specs=rows, check_vma=False
    )
```

```python
import functools
import math

import jax
import jax.numpy as jnp
from jax import lax
from jax.experimental import pallas as pl
from jax.experimental.pallas import tpu as pltpu
from jax.sharding import PartitionSpec as P

R_TWO = 2
R_FOUR = 4
R_PAIR = 8
R_FAR = 64

ROWS = 512
HEADS = 18
HEAD = 64
WIDTH = HEADS * HEAD
GROUPS = HEADS // 2
LANES = 128
SHARDS = 16
PAIR_ROWS = ROWS // R_PAIR
FAR_ROWS = ROWS // R_FAR
SCALE = HEAD**-0.5 * math.log2(math.e)
LOW = -1e30
EARLY = 2
FIRST_OWNER = SHARDS - GROUPS // 2

F32 = jnp.float32
BF16 = jnp.bfloat16


def iota(shape, dimension):
    return lax.broadcasted_iota(jnp.int32, shape, dimension)


def dot_t(a, b):
    return lax.dot_general(a, b, (((1,), (1,)), ((), ())), preferred_element_type=F32)


def dot(a, b):
    return lax.dot_general(a, b, (((1,), (0,)), ((), ())), preferred_element_type=F32)


def lane_offsets(ref, group, shape):
    first = iota(shape, len(shape) - 1) < HEAD
    return jnp.where(first, ref[2 * group], ref[2 * group + 1])


def split_heads(result, rows):
    first = iota((1, LANES), 1) < HEAD
    upper = jnp.where(first, result[:rows, :LANES], result[rows:, :LANES])
    lower = jnp.where(first, result[:rows, LANES:], result[rows:, LANES:])
    return upper, lower


def kernel(
    off_two_hbm, off_four_hbm, off_pair_hbm, off_far_hbm, q_hbm, k_hbm, v_hbm, out_ref,
    off_two, off_four, off_pair, off_far, q_ref, k_ref, v_ref,
    pair_send, pair_recv, q_pair, far_send, far_recv, back_send, back_recv, mixed, logs,
    load_sems, pair_send_sems, pair_recv_sems,
    far_send_sems, far_recv_sems, back_send_sems, back_recv_sems,
):
    me = lax.axis_index("seq")
    partner = me + 1 - 2 * lax.rem(me, 2)
    owned = lax.rem(me + SHARDS - FIRST_OWNER, SHARDS)
    is_owner = owned < GROUPS
    mine = jnp.minimum(owned, GROUPS - 1)
    partner_owns = lax.rem(partner + SHARDS - FIRST_OWNER, SHARDS) < GROUPS
    early = jnp.where(is_owner, EARLY, 0)
    greeted = GROUPS - is_owner.astype(jnp.int32) + 1 - partner_owns.astype(jnp.int32)

    barrier = pltpu.get_barrier_semaphore()

    @pl.when(is_owner)
    def _():
        for distance in range(1, SHARDS):
            pl.semaphore_signal(barrier, inc=1, device_id={"seq": lax.rem(me + distance, SHARDS)})

    @pl.when(jnp.logical_not(is_owner))
    def _():
        pl.semaphore_signal(barrier, inc=1, device_id={"seq": partner})

    loads = [
        pltpu.make_async_copy(source, target, load_sems.at[index])
        for index, (source, target) in enumerate(
            (
                (off_far_hbm, off_far),
                (off_pair_hbm, off_pair),
                (off_two_hbm, off_two),
                (off_four_hbm, off_four),
                (k_hbm, k_ref),
                (v_hbm, v_ref),
                (q_hbm, q_ref),
            )
        )
    ]
    for load in loads:
        load.start()

    def columns(group):
        return pl.ds(pl.multiple_of(group * LANES, LANES), LANES)

    def pair_copy(group):
        return pltpu.make_async_remote_copy(
            src_ref=pair_send.at[group],
            dst_ref=pair_recv.at[group],
            send_sem=pair_send_sems.at[group],
            recv_sem=pair_recv_sems.at[group],
            device_id={"seq": partner},
        )

    def far_copy(group, source):
        return pltpu.make_async_remote_copy(
            src_ref=far_send.at[group],
            dst_ref=far_recv.at[source],
            send_sem=far_send_sems.at[group],
            recv_sem=far_recv_sems.at[source],
            device_id={"seq": (FIRST_OWNER + group) % SHARDS},
        )

    def back_copy(group, target):
        return pltpu.make_async_remote_copy(
            src_ref=back_send.at[target],
            dst_ref=back_recv.at[group],
            send_sem=back_send_sems.at[target],
            recv_sem=back_recv_sems.at[group],
            device_id={"seq": target},
        )

    first_lanes = iota((1, LANES), 1) < HEAD
    head_lanes = [
        first_lanes.astype(F32).astype(BF16),
        (~first_lanes).astype(F32).astype(BF16),
    ]
    gather_pair = (iota((PAIR_ROWS, ROWS), 1) // R_PAIR == iota((PAIR_ROWS, ROWS), 0)).astype(F32).astype(BF16)
    gather_far = (iota((16, LANES), 1) // 16 == lax.rem(iota((16, LANES), 0), FAR_ROWS)).astype(F32).astype(BF16)

    def far_mask(group):
        shape = (R_FAR // 16, 16, LANES)
        rows = iota(shape, 0) * 16 + iota(shape, 1)
        return (rows == lane_offsets(off_far, group, shape)).astype(F32).astype(BF16)

    def pick_far(source, group, mask):
        shaped = source[:, columns(group)].reshape(FAR_ROWS, R_FAR // 16, 16, LANES) * mask[None]
        picked = (shaped[:, 0] + shaped[:, 1]) + (shaped[:, 2] + shaped[:, 3])
        return dot(gather_far, picked.reshape(FAR_ROWS * 16, LANES))

    def select_far(group):
        mask = far_mask(group)
        keys = pick_far(k_ref, group, mask)
        values = pick_far(v_ref, group, mask)
        queries = pick_far(q_ref, group, mask)
        low = iota((16, LANES), 0) < FAR_ROWS
        far_send[group, 0:16] = jnp.where(low, queries, keys).astype(BF16)
        far_send[group, 16:32] = values.astype(BF16)

    def pick_pair(source, group, mask):
        shaped = source[:, columns(group)].reshape(ROWS // 16, 16, LANES)
        return dot(gather_pair, (shaped * mask[None]).reshape(ROWS, LANES)).astype(BF16)

    def select_pair(group):
        offsets = lane_offsets(off_pair, group, (16, LANES))
        mask = (lax.rem(iota((16, LANES), 0), R_PAIR) == offsets).astype(F32).astype(BF16)
        pair_send[group, 0:PAIR_ROWS] = pick_pair(k_ref, group, mask)
        pair_send[group, PAIR_ROWS:] = pick_pair(v_ref, group, mask)
        q_pair[group] = pick_pair(q_ref, group, mask)

    def by_threes(work):
        def three(index, carry):
            for inner in range(3):
                work(index * 3 + inner)
            return carry

        lax.fori_loop(0, GROUPS // 3, three, 0)

    for load in loads:
        load.wait()
    by_threes(select_far)

    def send_far():
        for group in range(GROUPS):
            target = (FIRST_OWNER + group) % SHARDS

            @pl.when(me != target)
            def _():
                far_copy(group, me).start()

            @pl.when(me == target)
            def _():
                far_recv[me] = far_send[group]

    @pl.when(early == 0)
    def _():
        pl.semaphore_wait(barrier, greeted)
        send_far()

    by_threes(select_pair)

    def own():
        for distance in range(1, SHARDS):
            far_copy(0, lax.rem(me + distance, SHARDS)).wait_recv()
        both = far_recv[:, 0:16].astype(F32).reshape(SHARDS, 2, FAR_ROWS, LANES)
        queries = both[:, 0].reshape(SHARDS * FAR_ROWS, LANES).astype(BF16)
        keys = both[:, 1].reshape(SHARDS * FAR_ROWS, LANES).astype(BF16)
        values = far_recv[:, 16:32].astype(F32).reshape(SHARDS, 2, FAR_ROWS, LANES)[:, 0]
        values = values.reshape(SHARDS * FAR_ROWS, LANES).astype(BF16)
        values = jnp.concatenate([values, jnp.ones((SHARDS * FAR_ROWS, LANES), BF16)], axis=1)
        parts = []
        for parity in range(2):
            scores = dot_t(queries * head_lanes[parity], keys)
            highest = jnp.max(scores, axis=1, keepdims=True)
            weights = jnp.exp2((scores - highest) * SCALE).astype(BF16)
            result = dot(weights, values)
            parts.append((result[:, :LANES], result[:, LANES:], highest))
        upper, lower, highest = (jnp.where(first_lanes, a, b) for a, b in zip(*parts))
        result = (upper / lower).astype(BF16).astype(F32)
        log = highest * SCALE + jnp.log2(lower)
        coarse = log.astype(BF16).astype(F32)
        is_coarse = lax.rem(iota((1, LANES), 1), HEAD) < HEAD // 2
        log = jnp.where(is_coarse, coarse, log - coarse)
        shape = (SHARDS, 1, FAR_ROWS, LANES)
        both = jnp.concatenate([result.reshape(shape), log.reshape(shape)], axis=1)
        back_send[...] = both.reshape(SHARDS, 2 * FAR_ROWS, LANES).astype(BF16)
        for distance in range(1, SHARDS):
            back_copy(mine, lax.rem(me + distance, SHARDS)).start()
        back_recv[mine] = back_send[me]

    def dense(group):
        queries = q_ref[:, columns(group)]
        keys = k_ref[:, columns(group)]
        values = jnp.concatenate([v_ref[:, columns(group)], jnp.ones((ROWS, LANES), BF16)], axis=1)
        parts = []
        for parity in range(2):
            two = off_two[2 * group + parity]
            four = off_four[2 * group + parity]
            rows, cols = iota((8, LANES), 0), iota((8, LANES), 1)
            in_two = jnp.logical_and(rows % R_TWO == two, cols % R_TWO == two)
            in_four = jnp.logical_and(rows % R_FOUR == four, cols % R_FOUR == four)
            times = 1.0 + in_two.astype(F32) + in_four.astype(F32)
            times = jnp.concatenate([times] * (ROWS // LANES), axis=1)
            scores = dot_t(queries * head_lanes[parity], keys)
            highest = jnp.max(scores, axis=1, keepdims=True)
            raised = jnp.exp2((scores - highest) * SCALE)
            weights = (raised.reshape(ROWS // 8, 8, ROWS) * times[None]).reshape(ROWS, ROWS)
            result = dot(weights.astype(BF16), values)
            parts.append((result[:, :LANES], result[:, LANES:], highest))
        upper, lower, highest = (jnp.where(first_lanes, a, b) for a, b in zip(*parts))
        mixed[group] = upper / lower
        logs[group] = highest * SCALE + jnp.log2(lower)

    def step(group, carry):
        @pl.when(group == early)
        def _():
            @pl.when(early > 0)
            def _():
                pl.semaphore_wait(barrier, greeted)
                send_far()

            for chunk in range(GROUPS):
                pair_copy(chunk).start()

        dense(group)
        return carry

    lax.fori_loop(0, GROUPS, step, 0)

    def merge_pair(group):
        queries = q_pair[group]
        queries = jnp.concatenate([queries * head_lanes[0], queries * head_lanes[1]], axis=0)
        keys = jnp.concatenate([pair_send[group, 0:PAIR_ROWS], pair_recv[group, 0:PAIR_ROWS]], axis=0)
        values = jnp.concatenate([pair_send[group, PAIR_ROWS:], pair_recv[group, PAIR_ROWS:]], axis=0)
        values = jnp.concatenate([values, jnp.ones((2 * PAIR_ROWS, LANES), BF16)], axis=1)
        scores = dot_t(queries, keys)
        highest = jnp.max(scores, axis=1, keepdims=True)
        weights = jnp.exp2((scores - highest) * SCALE).astype(BF16)
        upper, lower = split_heads(dot(weights, values), PAIR_ROWS)
        highest = jnp.where(first_lanes, highest[:PAIR_ROWS], highest[PAIR_ROWS:])
        shape = (PAIR_ROWS, 8, LANES)
        result = (upper / lower).reshape(PAIR_ROWS, 1, LANES)
        log = (highest * SCALE + jnp.log2(lower)).reshape(PAIR_ROWS, 1, LANES)
        inside = iota((8, LANES), 0) == lane_offsets(off_pair, group, (8, LANES))
        result = jnp.broadcast_to(result, shape)
        log = jnp.where(inside[None], jnp.broadcast_to(log, shape), LOW)
        own_result = mixed[group].reshape(shape)
        own_log = logs[group].reshape(shape)
        peak = jnp.maximum(own_log, log)
        own_factor = jnp.exp2(own_log - peak)
        factor = jnp.exp2(log - peak)
        both = own_factor + factor
        mixed[group] = ((own_factor * own_result + factor * result) / both).reshape(ROWS, LANES)
        logs[group] = (peak + jnp.log2(both)).reshape(ROWS, LANES)

    def merge_three(index, carry):
        for inner in range(3):
            pair_copy(index * 3 + inner).wait_recv()
        for inner in range(3):
            merge_pair(index * 3 + inner)
        return carry

    def merge_and_own(index, carry):
        merge_three(index, carry)

        @pl.when(jnp.logical_and(is_owner, index == 0))
        def _():
            own()

        return carry

    lax.fori_loop(0, GROUPS // 3, merge_and_own, 0)

    for group in range(GROUPS):
        @pl.when(jnp.logical_or(jnp.logical_not(is_owner), mine != group))
        def _():
            back_copy(group, me).wait_recv()

    is_coarse = lax.rem(iota((1, LANES), 1), HEAD) < HEAD // 2

    def merge_far(group):
        both = back_recv[group].astype(F32)
        result, log = both[:FAR_ROWS], both[FAR_ROWS:]
        log = log + jnp.where(is_coarse, pltpu.roll(log, LANES - HEAD // 2, 1), pltpu.roll(log, HEAD // 2, 1))
        shape = (FAR_ROWS, R_FAR // 8, 8, LANES)
        row = (FAR_ROWS, 1, 8, LANES)
        result = jnp.broadcast_to(result.reshape(FAR_ROWS, 1, LANES), (FAR_ROWS, 8, LANES)).reshape(row)
        log = jnp.broadcast_to(log.reshape(FAR_ROWS, 1, LANES), (FAR_ROWS, 8, LANES)).reshape(row)
        phase = iota((R_FAR // 8, 8, LANES), 0) * 8 + iota((R_FAR // 8, 8, LANES), 1)
        inside = phase == lane_offsets(off_far, group, (R_FAR // 8, 8, LANES))
        own_result = mixed[group].reshape(shape)
        own_log = logs[group].reshape(shape)
        share = jnp.where(inside[None], 1.0 / (1.0 + jnp.exp2(own_log - log)), 0.0)
        merged = own_result + share * (result - own_result)
        out_ref[:, columns(group)] = merged.reshape(ROWS, LANES).astype(BF16)

    by_threes(merge_far)

    for group in range(GROUPS):
        pair_copy(group).wait_send()

        @pl.when(me != (FIRST_OWNER + group) % SHARDS)
        def _():
            far_copy(group, me).wait_send()

    @pl.when(is_owner)
    def _():
        for distance in range(1, SHARDS):
            back_copy(mine, lax.rem(me + distance, SHARDS)).wait_send()


def local(queries, key_rows, value_rows, offset_two, offset_four, offset_pair, offset_far):
    anywhere = pl.BlockSpec(memory_space=pl.ANY)
    return pl.pallas_call(
        kernel,
        out_shape=jax.ShapeDtypeStruct((ROWS, WIDTH), BF16),
        in_specs=[anywhere] * 7,
        out_specs=pl.BlockSpec(memory_space=pltpu.VMEM),
        scratch_shapes=[
            *[pltpu.SMEM((HEADS,), jnp.int32)] * 4,
            *[pltpu.VMEM((ROWS, WIDTH), BF16)] * 3,
            pltpu.VMEM((GROUPS, 2 * PAIR_ROWS, LANES), BF16),
            pltpu.VMEM((GROUPS, 2 * PAIR_ROWS, LANES), BF16),
            pltpu.VMEM((GROUPS, PAIR_ROWS, LANES), BF16),
            pltpu.VMEM((GROUPS, 32, LANES), BF16),
            pltpu.VMEM((SHARDS, 32, LANES), BF16),
            pltpu.VMEM((SHARDS, 16, LANES), BF16),
            pltpu.VMEM((GROUPS, 16, LANES), BF16),
            pltpu.VMEM((GROUPS, ROWS, LANES), F32),
            pltpu.VMEM((GROUPS, ROWS, LANES), F32),
            pltpu.SemaphoreType.DMA((7,)),
            pltpu.SemaphoreType.DMA((GROUPS,)),
            pltpu.SemaphoreType.DMA((GROUPS,)),
            pltpu.SemaphoreType.DMA((GROUPS,)),
            pltpu.SemaphoreType.DMA((SHARDS,)),
            pltpu.SemaphoreType.DMA((SHARDS,)),
            pltpu.SemaphoreType.DMA((GROUPS,)),
        ],
        compiler_params=pltpu.CompilerParams(
            collective_id=0, has_side_effects=True, vmem_limit_bytes=56 * 1024 * 1024
        ),
        cost_estimate=pl.CostEstimate(flops=2 * 10**9, bytes_accessed=5 * 10**6, transcendentals=6 * 10**6),
        name="dilated_attention",
    )(offset_two, offset_four, offset_pair, offset_far, queries, key_rows, value_rows)


def solution(mesh):
    rows = P(("dp", "seq"), None)
    return jax.shard_map(
        local, mesh=mesh, in_specs=(rows,) * 3 + (P(),) * 4, out_specs=rows, check_vma=False
    )
```

```python
import functools
import math

import jax
import jax.numpy as jnp
from jax import lax
from jax.experimental import pallas as pl
from jax.experimental.pallas import tpu as pltpu
from jax.sharding import PartitionSpec as P

R_TWO = 2
R_FOUR = 4
R_PAIR = 8
R_FAR = 64

ROWS = 512
HEADS = 18
HEAD = 64
WIDTH = HEADS * HEAD
GROUPS = HEADS // 2
LANES = 128
SHARDS = 16
PAIR_ROWS = ROWS // R_PAIR
FAR_ROWS = ROWS // R_FAR
SCALE = HEAD**-0.5 * math.log2(math.e)
LOW = -1e30
EARLY = 1
OWNERS = (14, 15, 0, 1, 2)
SLAB = 2 * LANES
NEAREST = sorted(range(SHARDS), key=lambda each: min(each, SHARDS - each))

F32 = jnp.float32
BF16 = jnp.bfloat16


def iota(shape, dimension):
    return lax.broadcasted_iota(jnp.int32, shape, dimension)


def dot_t(a, b):
    return lax.dot_general(a, b, (((1,), (1,)), ((), ())), preferred_element_type=F32)


def dot(a, b):
    return lax.dot_general(a, b, (((1,), (0,)), ((), ())), preferred_element_type=F32)


def lane_offsets(ref, group, shape):
    first = iota(shape, len(shape) - 1) < HEAD
    return jnp.where(first, ref[2 * group], ref[2 * group + 1])


def split_heads(result, rows):
    first = iota((1, LANES), 1) < HEAD
    upper = jnp.where(first, result[:rows, :LANES], result[rows:, :LANES])
    lower = jnp.where(first, result[:rows, LANES:], result[rows:, LANES:])
    return upper, lower


def kernel(
    off_two_hbm, off_four_hbm, off_pair_hbm, off_far_hbm, q_hbm, k_hbm, v_hbm, out_ref,
    off_two, off_four, off_pair, off_far, q_ref, k_ref, v_ref,
    pair_send, pair_recv, q_pair, far_send, far_recv, back_send, back_recv, mixed, logs, at_far,
    offset_sems, load_sems, pair_send_sems, pair_recv_sems,
    far_send_sems, far_recv_sems, back_send_sems, back_recv_sems,
):
    me = lax.axis_index("seq")
    partner = me + 1 - 2 * lax.rem(me, 2)
    is_owner, partner_owns = False, False
    mine = 0
    for index, owner in enumerate(OWNERS):
        is_owner = jnp.logical_or(is_owner, me == owner)
        partner_owns = jnp.logical_or(partner_owns, partner == owner)
        mine = jnp.where(me == owner, index, mine)
    group_count = jnp.where(is_owner, jnp.minimum(GROUPS - 2 * mine, 2), 0)
    early = jnp.where(is_owner, EARLY, 0)
    greeted = len(OWNERS) - is_owner.astype(jnp.int32) + 1 - partner_owns.astype(jnp.int32)

    barrier = pltpu.get_barrier_semaphore()

    @pl.when(is_owner)
    def _():
        for distance in range(1, SHARDS):
            pl.semaphore_signal(barrier, inc=1, device_id={"seq": lax.rem(me + distance, SHARDS)})

    @pl.when(jnp.logical_not(is_owner))
    def _():
        pl.semaphore_signal(barrier, inc=1, device_id={"seq": partner})

    offset_loads = [
        pltpu.make_async_copy(source, target, offset_sems.at[index])
        for index, (source, target) in enumerate(
            ((off_far_hbm, off_far), (off_pair_hbm, off_pair), (off_two_hbm, off_two), (off_four_hbm, off_four))
        )
    ]

    def slab_loads(index):
        part = pl.ds(index * SLAB, min(SLAB, WIDTH - index * SLAB))
        return [
            pltpu.make_async_copy(source.at[:, part], target.at[:, part], load_sems.at[which, index])
            for which, (source, target) in enumerate(((q_hbm, q_ref), (k_hbm, k_ref), (v_hbm, v_ref)))
        ]

    for load in offset_loads:
        load.start()
    for index in range(len(OWNERS)):
        for load in slab_loads(index):
            load.start()

    def columns(group):
        start = group * LANES
        return pl.ds(start if isinstance(group, int) else pl.multiple_of(start, LANES), LANES)

    def pair_copy(group):
        return pltpu.make_async_remote_copy(
            src_ref=pair_send.at[group],
            dst_ref=pair_recv.at[group],
            send_sem=pair_send_sems.at[group],
            recv_sem=pair_recv_sems.at[group],
            device_id={"seq": partner},
        )

    def far_copy(index, source):
        rows = pl.ds(0, 48 if 2 * index + 1 < GROUPS else 32)
        return pltpu.make_async_remote_copy(
            src_ref=far_send.at[index, rows],
            dst_ref=far_recv.at[source, rows],
            send_sem=far_send_sems.at[index],
            recv_sem=far_recv_sems.at[source],
            device_id={"seq": OWNERS[index]},
        )

    def back_copy(index, target):
        return pltpu.make_async_remote_copy(
            src_ref=back_send.at[target],
            dst_ref=back_recv.at[index],
            send_sem=back_send_sems.at[target],
            recv_sem=back_recv_sems.at[index],
            device_id={"seq": target},
        )

    first_lanes = iota((1, LANES), 1) < HEAD
    head_lanes = [
        first_lanes.astype(F32).astype(BF16),
        (~first_lanes).astype(F32).astype(BF16),
    ]
    gather_pair = (iota((PAIR_ROWS, ROWS), 1) // R_PAIR == iota((PAIR_ROWS, ROWS), 0)).astype(F32).astype(BF16)
    gather_far = (iota((16, LANES), 1) // 16 == lax.rem(iota((16, LANES), 0), FAR_ROWS)).astype(F32).astype(BF16)

    def far_mask(group):
        shape = (R_FAR // 16, 16, LANES)
        rows = iota(shape, 0) * 16 + iota(shape, 1)
        return (rows == lane_offsets(off_far, group, shape)).astype(F32).astype(BF16)

    def pick_far(source, group, mask):
        shaped = source[:, columns(group)].reshape(FAR_ROWS, R_FAR // 16, 16, LANES) * mask[None]
        picked = (shaped[:, 0] + shaped[:, 1]) + (shaped[:, 2] + shaped[:, 3])
        return dot(gather_far, picked.reshape(FAR_ROWS * 16, LANES))

    def select_far(index):
        low = iota((16, LANES), 0) < FAR_ROWS
        picked = []
        for group in range(2 * index, min(2 * index + 2, GROUPS)):
            mask = far_mask(group)
            picked += [pick_far(source, group, mask) for source in (q_ref, k_ref, v_ref)]
        picked += picked[-1:] * (len(picked) % 2)
        for tile in range(len(picked) // 2):
            both = jnp.where(low, picked[2 * tile], picked[2 * tile + 1])
            far_send[index, 16 * tile : 16 * tile + 16] = both.astype(BF16)

    def pick_pair(source, group, mask):
        shaped = source[:, columns(group)].reshape(ROWS // 16, 16, LANES)
        return dot(gather_pair, (shaped * mask[None]).reshape(ROWS, LANES)).astype(BF16)

    def select_pair(group):
        offsets = lane_offsets(off_pair, group, (16, LANES))
        mask = (lax.rem(iota((16, LANES), 0), R_PAIR) == offsets).astype(F32).astype(BF16)
        pair_send[group, 0:PAIR_ROWS] = pick_pair(k_ref, group, mask)
        pair_send[group, PAIR_ROWS:] = pick_pair(v_ref, group, mask)
        q_pair[group] = pick_pair(q_ref, group, mask)

    def by_threes(work):
        def three(index, carry):
            for inner in range(3):
                work(index * 3 + inner)
            return carry

        lax.fori_loop(0, GROUPS // 3, three, 0)

    def send_far(index):
        @pl.when(me != OWNERS[index])
        def _():
            far_copy(index, me).start()

        @pl.when(me == OWNERS[index])
        def _():
            far_recv[me] = far_send[index]

    @pl.when(early == 0)
    def _():
        pl.semaphore_wait(barrier, greeted)

    for load in offset_loads:
        load.wait()
    for index in range(len(OWNERS)):
        for load in slab_loads(index):
            load.wait()
        select_far(index)

        @pl.when(early == 0)
        def _():
            send_far(index)

    by_threes(select_pair)

    def own(slot, carry):
        parts = []
        for part in range(3):
            place = 3 * slot + part
            start = pl.multiple_of(place // 2 * 16, 16)
            tile = far_recv[:, pl.ds(start, 16)].astype(F32).reshape(SHARDS, 2, FAR_ROWS, LANES)
            rows = jnp.where(lax.rem(place, 2) == 0, tile[:, 0], tile[:, 1])
            parts.append(rows.reshape(SHARDS * FAR_ROWS, LANES).astype(BF16))
        queries, keys, values = parts
        values = jnp.concatenate([values, jnp.ones((SHARDS * FAR_ROWS, LANES), BF16)], axis=1)
        parts = []
        for parity in range(2):
            scores = dot_t(queries * head_lanes[parity], keys)
            highest = jnp.max(scores, axis=1, keepdims=True)
            weights = jnp.exp2((scores - highest) * SCALE).astype(BF16)
            result = dot(weights, values)
            parts.append((result[:, :LANES], result[:, LANES:], highest))
        upper, lower, highest = (jnp.where(first_lanes, a, b) for a, b in zip(*parts))
        result = (upper / lower).astype(BF16).astype(F32)
        log = highest * SCALE + jnp.log2(lower)
        coarse = log.astype(BF16).astype(F32)
        is_coarse = lax.rem(iota((1, LANES), 1), HEAD) < HEAD // 2
        log = jnp.where(is_coarse, coarse, log - coarse)
        shape = (SHARDS, 1, FAR_ROWS, LANES)
        both = jnp.concatenate([result.reshape(shape), log.reshape(shape)], axis=1)
        rows = pl.ds(pl.multiple_of(slot * 16, 16), 16)
        back_send[:, rows] = both.reshape(SHARDS, 2 * FAR_ROWS, LANES).astype(BF16)
        return carry

    def own_all():
        for distance in range(1, SHARDS):
            source = lax.rem(me + distance, SHARDS)

            @pl.when(group_count == 2)
            def _():
                far_copy(0, source).wait_recv()

            @pl.when(group_count == 1)
            def _():
                far_copy(len(OWNERS) - 1, source).wait_recv()

        lax.fori_loop(0, group_count, own, 0)
        for target in NEAREST:
            @pl.when(me != target)
            def _():
                back_copy(mine, target).start()

        back_recv[mine] = back_send[me]

    def dense(group):
        queries = q_ref[:, columns(group)]
        keys = k_ref[:, columns(group)]
        values = jnp.concatenate([v_ref[:, columns(group)], jnp.ones((ROWS, LANES), BF16)], axis=1)
        parts = []
        for parity in range(2):
            two = off_two[2 * group + parity]
            four = off_four[2 * group + parity]
            rows, cols = iota((8, LANES), 0), iota((8, LANES), 1)
            in_two = jnp.logical_and(rows % R_TWO == two, cols % R_TWO == two)
            in_four = jnp.logical_and(rows % R_FOUR == four, cols % R_FOUR == four)
            times = 1.0 + in_two.astype(F32) + in_four.astype(F32)
            times = jnp.concatenate([times] * (ROWS // LANES), axis=1)
            scores = dot_t(queries * head_lanes[parity], keys)
            highest = jnp.max(scores, axis=1, keepdims=True)
            raised = jnp.exp2((scores - highest) * SCALE)
            weights = (raised.reshape(ROWS // 8, 8, ROWS) * times[None]).reshape(ROWS, ROWS)
            result = dot(weights.astype(BF16), values)
            parts.append((result[:, :LANES], result[:, LANES:], highest))
        upper, lower, highest = (jnp.where(first_lanes, a, b) for a, b in zip(*parts))
        mixed[group] = upper / lower
        logs[group] = highest * SCALE + jnp.log2(lower)

    def step(group, carry):
        @pl.when(group == early)
        def _():
            @pl.when(early > 0)
            def _():
                pl.semaphore_wait(barrier, greeted)
                for index in range(len(OWNERS)):
                    send_far(index)

            for chunk in range(GROUPS):
                pair_copy(chunk).start()

        dense(group)
        return carry

    lax.fori_loop(0, GROUPS, step, 0)

    def far_inside(group):
        shape = (R_FAR // 8, 8, LANES)
        return iota(shape, 0) * 8 + iota(shape, 1) == lane_offsets(off_far, group, shape)

    def merge_pair(group):
        queries = q_pair[group]
        queries = jnp.concatenate([queries * head_lanes[0], queries * head_lanes[1]], axis=0)
        keys = jnp.concatenate([pair_send[group, 0:PAIR_ROWS], pair_recv[group, 0:PAIR_ROWS]], axis=0)
        values = jnp.concatenate([pair_send[group, PAIR_ROWS:], pair_recv[group, PAIR_ROWS:]], axis=0)
        values = jnp.concatenate([values, jnp.ones((2 * PAIR_ROWS, LANES), BF16)], axis=1)
        scores = dot_t(queries, keys)
        highest = jnp.max(scores, axis=1, keepdims=True)
        weights = jnp.exp2((scores - highest) * SCALE).astype(BF16)
        upper, lower = split_heads(dot(weights, values), PAIR_ROWS)
        highest = jnp.where(first_lanes, highest[:PAIR_ROWS], highest[PAIR_ROWS:])
        shape = (PAIR_ROWS, 8, LANES)
        result = (upper / lower).reshape(PAIR_ROWS, 1, LANES)
        log = (highest * SCALE + jnp.log2(lower)).reshape(PAIR_ROWS, 1, LANES)
        inside = iota((8, LANES), 0) == lane_offsets(off_pair, group, (8, LANES))
        result = jnp.broadcast_to(result, shape)
        log = jnp.where(inside[None], jnp.broadcast_to(log, shape), LOW)
        own_result = mixed[group].reshape(shape)
        own_log = logs[group].reshape(shape)
        peak = jnp.maximum(own_log, log)
        own_factor = jnp.exp2(own_log - peak)
        factor = jnp.exp2(log - peak)
        both = own_factor + factor
        merged = (own_factor * own_result + factor * result) / both
        log = peak + jnp.log2(both)
        out_ref[:, columns(group)] = merged.reshape(ROWS, LANES).astype(BF16)
        shape = (FAR_ROWS, R_FAR // 8, 8, LANES)
        inside = far_inside(group)
        for place, each in enumerate((merged, log)):
            kept = jnp.where(inside[None], each.reshape(shape), 0.0)
            at_far[group, place] = jnp.sum(jnp.sum(kept, axis=1), axis=1)

    def merge_three(index, carry):
        for inner in range(3):
            pair_copy(index * 3 + inner).wait_recv()
        for inner in range(3):
            merge_pair(index * 3 + inner)
        return carry

    def merge_and_own(index, carry):
        merge_three(index, carry)

        @pl.when(jnp.logical_and(is_owner, index == 0))
        def _():
            own_all()

        return carry

    lax.fori_loop(0, GROUPS // 3, merge_and_own, 0)

    for index in range(len(OWNERS)):
        @pl.when(me != OWNERS[index])
        def _():
            back_copy(index, me).wait_recv()

    is_coarse = lax.rem(iota((1, LANES), 1), HEAD) < HEAD // 2

    def merge_far(group):
        rows = 16 * (group % 2)
        both = back_recv[group // 2, rows : rows + 16].astype(F32)
        result, log = both[:FAR_ROWS], both[FAR_ROWS:]
        log = log + jnp.where(is_coarse, pltpu.roll(log, LANES - HEAD // 2, 1), pltpu.roll(log, HEAD // 2, 1))
        own_result, own_log = at_far[group, 0], at_far[group, 1]
        peak = jnp.maximum(own_log, log)
        own_factor = jnp.exp2(own_log - peak)
        factor = jnp.exp2(log - peak)
        merged = (own_factor * own_result + factor * result) / (own_factor + factor)
        merged = jnp.broadcast_to(merged.reshape(FAR_ROWS, 1, LANES), (FAR_ROWS, 16, LANES)).astype(BF16)
        mask = far_mask(group)
        earlier = out_ref[:, columns(group)].reshape(FAR_ROWS, R_FAR // 16, 16, LANES)
        final = earlier * (jnp.ones((), BF16) - mask)[None] + merged[:, None] * mask[None]
        out_ref[:, columns(group)] = final.reshape(ROWS, LANES)

    for group in range(GROUPS):
        merge_far(group)

    for index in range(len(OWNERS)):
        @pl.when(me != OWNERS[index])
        def _():
            far_copy(index, me).wait_send()

    for group in range(GROUPS):
        pair_copy(group).wait_send()

    @pl.when(is_owner)
    def _():
        for distance in range(1, SHARDS):
            back_copy(0, lax.rem(me + distance, SHARDS)).wait_send()


def local(queries, key_rows, value_rows, offset_two, offset_four, offset_pair, offset_far):
    anywhere = pl.BlockSpec(memory_space=pl.ANY)
    return pl.pallas_call(
        kernel,
        out_shape=jax.ShapeDtypeStruct((ROWS, WIDTH), BF16),
        in_specs=[anywhere] * 7,
        out_specs=pl.BlockSpec(memory_space=pltpu.VMEM),
        scratch_shapes=[
            *[pltpu.SMEM((HEADS,), jnp.int32)] * 4,
            *[pltpu.VMEM((ROWS, WIDTH), BF16)] * 3,
            pltpu.VMEM((GROUPS, 2 * PAIR_ROWS, LANES), BF16),
            pltpu.VMEM((GROUPS, 2 * PAIR_ROWS, LANES), BF16),
            pltpu.VMEM((GROUPS, PAIR_ROWS, LANES), BF16),
            pltpu.VMEM((len(OWNERS), 48, LANES), BF16),
            pltpu.VMEM((SHARDS, 48, LANES), BF16),
            pltpu.VMEM((SHARDS, 32, LANES), BF16),
            pltpu.VMEM((len(OWNERS), 32, LANES), BF16),
            pltpu.VMEM((GROUPS, ROWS, LANES), F32),
            pltpu.VMEM((GROUPS, ROWS, LANES), F32),
            pltpu.VMEM((GROUPS, 2, FAR_ROWS, LANES), F32),
            pltpu.SemaphoreType.DMA((4,)),
            pltpu.SemaphoreType.DMA((3, len(OWNERS))),
            pltpu.SemaphoreType.DMA((GROUPS,)),
            pltpu.SemaphoreType.DMA((GROUPS,)),
            pltpu.SemaphoreType.DMA((len(OWNERS),)),
            pltpu.SemaphoreType.DMA((SHARDS,)),
            pltpu.SemaphoreType.DMA((SHARDS,)),
            pltpu.SemaphoreType.DMA((len(OWNERS),)),
        ],
        compiler_params=pltpu.CompilerParams(
            collective_id=0, has_side_effects=True, vmem_limit_bytes=56 * 1024 * 1024
        ),
        cost_estimate=pl.CostEstimate(flops=2 * 10**9, bytes_accessed=5 * 10**6, transcendentals=6 * 10**6),
        name="dilated_attention",
    )(offset_two, offset_four, offset_pair, offset_far, queries, key_rows, value_rows)


def solution(mesh):
    rows = P(("dp", "seq"), None)
    return jax.shard_map(
        local, mesh=mesh, in_specs=(rows,) * 3 + (P(),) * 4, out_specs=rows, check_vma=False
    )
```

```python
import functools
import math

import jax
import jax.numpy as jnp
from jax import lax
from jax.experimental import pallas as pl
from jax.experimental.pallas import tpu as pltpu
from jax.sharding import PartitionSpec as P

R_TWO = 2
R_FOUR = 4
R_PAIR = 8
R_FAR = 64

ROWS = 512
HEADS = 18
HEAD = 64
WIDTH = HEADS * HEAD
GROUPS = HEADS // 2
LANES = 128
SHARDS = 16
PAIR_ROWS = ROWS // R_PAIR
FAR_ROWS = ROWS // R_FAR
SCALE = HEAD**-0.5 * math.log2(math.e)
LOW = -1e30
EARLY = 1
PAIR_OWNER = 1
PAIR_OTHER = 0
OWNERS = (14, 15, 0, 1, 2)
SLAB = 2 * LANES
NEAREST = sorted(range(SHARDS), key=lambda each: min(each, SHARDS - each))

F32 = jnp.float32
BF16 = jnp.bfloat16


def iota(shape, dimension):
    return lax.broadcasted_iota(jnp.int32, shape, dimension)


def dot_t(a, b):
    return lax.dot_general(a, b, (((1,), (1,)), ((), ())), preferred_element_type=F32)


def dot(a, b):
    return lax.dot_general(a, b, (((1,), (0,)), ((), ())), preferred_element_type=F32)


def lane_offsets(ref, group, shape):
    first = iota(shape, len(shape) - 1) < HEAD
    return jnp.where(first, ref[2 * group], ref[2 * group + 1])


def split_heads(result, rows):
    first = iota((1, LANES), 1) < HEAD
    upper = jnp.where(first, result[:rows, :LANES], result[rows:, :LANES])
    lower = jnp.where(first, result[:rows, LANES:], result[rows:, LANES:])
    return upper, lower


def kernel(
    off_two_hbm, off_four_hbm, off_pair_hbm, off_far_hbm, q_hbm, k_hbm, v_hbm, out_ref,
    off_two, off_four, off_pair, off_far, q_ref, k_ref, v_ref,
    pair_send, pair_recv, q_pair, far_send, far_recv, back_send, back_recv, mixed, logs, at_far,
    offset_sems, load_sems, pair_send_sems, pair_recv_sems,
    far_send_sems, far_recv_sems, back_send_sems, back_recv_sems,
):
    me = lax.axis_index("seq")
    partner = me + 1 - 2 * lax.rem(me, 2)
    is_owner, partner_owns = False, False
    mine = 0
    for index, owner in enumerate(OWNERS):
        is_owner = jnp.logical_or(is_owner, me == owner)
        partner_owns = jnp.logical_or(partner_owns, partner == owner)
        mine = jnp.where(me == owner, index, mine)
    group_count = jnp.where(is_owner, jnp.minimum(GROUPS - 2 * mine, 2), 0)
    early = jnp.where(is_owner, EARLY, 0)
    greeted = len(OWNERS) - is_owner.astype(jnp.int32) + 1 - partner_owns.astype(jnp.int32)

    barrier = pltpu.get_barrier_semaphore()

    @pl.when(is_owner)
    def _():
        for distance in range(1, SHARDS):
            pl.semaphore_signal(barrier, inc=1, device_id={"seq": lax.rem(me + distance, SHARDS)})

    @pl.when(jnp.logical_not(is_owner))
    def _():
        pl.semaphore_signal(barrier, inc=1, device_id={"seq": partner})

    offset_loads = [
        pltpu.make_async_copy(source, target, offset_sems.at[index])
        for index, (source, target) in enumerate(
            ((off_far_hbm, off_far), (off_pair_hbm, off_pair), (off_two_hbm, off_two), (off_four_hbm, off_four))
        )
    ]

    def slab_loads(index):
        part = pl.ds(index * SLAB, min(SLAB, WIDTH - index * SLAB))
        return [
            pltpu.make_async_copy(source.at[:, part], target.at[:, part], load_sems.at[which, index])
            for which, (source, target) in enumerate(((q_hbm, q_ref), (k_hbm, k_ref), (v_hbm, v_ref)))
        ]

    for load in offset_loads:
        load.start()
    for index in range(len(OWNERS)):
        for load in slab_loads(index):
            load.start()

    def columns(group):
        start = group * LANES
        return pl.ds(start if isinstance(group, int) else pl.multiple_of(start, LANES), LANES)

    def pair_copy(group):
        return pltpu.make_async_remote_copy(
            src_ref=pair_send.at[group],
            dst_ref=pair_recv.at[group],
            send_sem=pair_send_sems.at[group],
            recv_sem=pair_recv_sems.at[group],
            device_id={"seq": partner},
        )

    def far_copy(index, source):
        rows = pl.ds(0, 48 if 2 * index + 1 < GROUPS else 32)
        return pltpu.make_async_remote_copy(
            src_ref=far_send.at[index, rows],
            dst_ref=far_recv.at[source, rows],
            send_sem=far_send_sems.at[index],
            recv_sem=far_recv_sems.at[source],
            device_id={"seq": OWNERS[index]},
        )

    def back_copy(index, target):
        return pltpu.make_async_remote_copy(
            src_ref=back_send.at[target],
            dst_ref=back_recv.at[index],
            send_sem=back_send_sems.at[target],
            recv_sem=back_recv_sems.at[index],
            device_id={"seq": target},
        )

    first_lanes = iota((1, LANES), 1) < HEAD
    head_lanes = [
        first_lanes.astype(F32).astype(BF16),
        (~first_lanes).astype(F32).astype(BF16),
    ]
    gather_pair = (iota((PAIR_ROWS, ROWS), 1) // R_PAIR == iota((PAIR_ROWS, ROWS), 0)).astype(F32).astype(BF16)
    gather_far = (iota((16, LANES), 1) // 16 == lax.rem(iota((16, LANES), 0), FAR_ROWS)).astype(F32).astype(BF16)

    def far_mask(group):
        shape = (R_FAR // 16, 16, LANES)
        rows = iota(shape, 0) * 16 + iota(shape, 1)
        return (rows == lane_offsets(off_far, group, shape)).astype(F32).astype(BF16)

    def pick_far(source, group, mask):
        shaped = source[:, columns(group)].reshape(FAR_ROWS, R_FAR // 16, 16, LANES) * mask[None]
        picked = (shaped[:, 0] + shaped[:, 1]) + (shaped[:, 2] + shaped[:, 3])
        return dot(gather_far, picked.reshape(FAR_ROWS * 16, LANES))

    def select_far(index):
        low = iota((16, LANES), 0) < FAR_ROWS
        picked = []
        for group in range(2 * index, min(2 * index + 2, GROUPS)):
            mask = far_mask(group)
            picked += [pick_far(source, group, mask) for source in (q_ref, k_ref, v_ref)]
        picked += picked[-1:] * (len(picked) % 2)
        for tile in range(len(picked) // 2):
            both = jnp.where(low, picked[2 * tile], picked[2 * tile + 1])
            far_send[index, 16 * tile : 16 * tile + 16] = both.astype(BF16)

    def pick_pair(source, group, mask):
        shaped = source[:, columns(group)].reshape(ROWS // 16, 16, LANES)
        return dot(gather_pair, (shaped * mask[None]).reshape(ROWS, LANES)).astype(BF16)

    def select_pair(group):
        offsets = lane_offsets(off_pair, group, (16, LANES))
        mask = (lax.rem(iota((16, LANES), 0), R_PAIR) == offsets).astype(F32).astype(BF16)
        pair_send[group, 0:PAIR_ROWS] = pick_pair(k_ref, group, mask)
        pair_send[group, PAIR_ROWS:] = pick_pair(v_ref, group, mask)
        q_pair[group] = pick_pair(q_ref, group, mask)

    def by_threes(work):
        def three(index, carry):
            for inner in range(3):
                work(index * 3 + inner)
            return carry

        lax.fori_loop(0, GROUPS // 3, three, 0)

    def send_far(index):
        @pl.when(me != OWNERS[index])
        def _():
            far_copy(index, me).start()

        @pl.when(me == OWNERS[index])
        def _():
            far_recv[me] = far_send[index]

    @pl.when(early == 0)
    def _():
        pl.semaphore_wait(barrier, greeted)

    for load in offset_loads:
        load.wait()
    for index in range(len(OWNERS)):
        for load in slab_loads(index):
            load.wait()
        select_far(index)

        @pl.when(early == 0)
        def _():
            send_far(index)

    by_threes(select_pair)

    def own(slot):
        parts = []
        for part in range(3):
            place = 3 * slot + part
            start = place // 2 * 16
            tile = far_recv[:, start : start + 16].astype(F32).reshape(SHARDS, 2, FAR_ROWS, LANES)
            parts.append(tile[:, place % 2].reshape(SHARDS * FAR_ROWS, LANES).astype(BF16))
        queries, keys, values = parts
        values = jnp.concatenate([values, jnp.ones((SHARDS * FAR_ROWS, LANES), BF16)], axis=1)
        parts = []
        for parity in range(2):
            scores = dot_t(queries * head_lanes[parity], keys)
            highest = jnp.max(scores, axis=1, keepdims=True)
            weights = jnp.exp2((scores - highest) * SCALE).astype(BF16)
            result = dot(weights, values)
            parts.append((result[:, :LANES], result[:, LANES:], highest))
        upper, lower, highest = (jnp.where(first_lanes, a, b) for a, b in zip(*parts))
        result = (upper / lower).astype(BF16).astype(F32)
        log = highest * SCALE + jnp.log2(lower)
        coarse = log.astype(BF16).astype(F32)
        is_coarse = lax.rem(iota((1, LANES), 1), HEAD) < HEAD // 2
        log = jnp.where(is_coarse, coarse, log - coarse)
        shape = (SHARDS, 1, FAR_ROWS, LANES)
        both = jnp.concatenate([result.reshape(shape), log.reshape(shape)], axis=1)
        return both.reshape(SHARDS, 2 * FAR_ROWS, LANES).astype(BF16)

    def own_all():
        for distance in range(1, SHARDS):
            source = lax.rem(me + distance, SHARDS)

            @pl.when(group_count == 2)
            def _():
                far_copy(0, source).wait_recv()

            @pl.when(group_count == 1)
            def _():
                far_copy(len(OWNERS) - 1, source).wait_recv()

        @pl.when(group_count == 2)
        def _():
            results = [own(0), own(1)]
            for slot, result in enumerate(results):
                back_send[:, 16 * slot : 16 * slot + 16] = result

        @pl.when(group_count == 1)
        def _():
            back_send[:, 0:16] = own(0)

        for target in NEAREST:
            @pl.when(me != target)
            def _():
                back_copy(mine, target).start()

        back_recv[mine] = back_send[me]

    def dense(group):
        queries = q_ref[:, columns(group)]
        keys = k_ref[:, columns(group)]
        values = jnp.concatenate([v_ref[:, columns(group)], jnp.ones((ROWS, LANES), BF16)], axis=1)
        parts = []
        for parity in range(2):
            two = off_two[2 * group + parity]
            four = off_four[2 * group + parity]
            rows, cols = iota((8, LANES), 0), iota((8, LANES), 1)
            in_two = jnp.logical_and(rows % R_TWO == two, cols % R_TWO == two)
            in_four = jnp.logical_and(rows % R_FOUR == four, cols % R_FOUR == four)
            times = 1.0 + in_two.astype(F32) + in_four.astype(F32)
            times = jnp.concatenate([times] * (ROWS // LANES), axis=1)
            scores = dot_t(queries * head_lanes[parity], keys)
            highest = jnp.max(scores, axis=1, keepdims=True)
            raised = jnp.exp2((scores - highest) * SCALE)
            weights = (raised.reshape(ROWS // 8, 8, ROWS) * times[None]).reshape(ROWS, ROWS)
            result = dot(weights.astype(BF16), values)
            parts.append((result[:, :LANES], result[:, LANES:], highest))
        upper, lower, highest = (jnp.where(first_lanes, a, b) for a, b in zip(*parts))
        mixed[group] = upper / lower
        logs[group] = highest * SCALE + jnp.log2(lower)

    def step(group, carry):
        @pl.when(group == early)
        def _():
            @pl.when(early > 0)
            def _():
                pl.semaphore_wait(barrier, greeted)
                for index in range(len(OWNERS)):
                    send_far(index)

        @pl.when(group == jnp.where(is_owner, PAIR_OWNER, PAIR_OTHER))
        def _():
            for chunk in range(GROUPS):
                pair_copy(chunk).start()

        dense(group)
        return carry

    lax.fori_loop(0, GROUPS, step, 0)

    def far_inside(group):
        shape = (R_FAR // 8, 8, LANES)
        return iota(shape, 0) * 8 + iota(shape, 1) == lane_offsets(off_far, group, shape)

    def merge_pair(group):
        queries = q_pair[group]
        queries = jnp.concatenate([queries * head_lanes[0], queries * head_lanes[1]], axis=0)
        keys = jnp.concatenate([pair_send[group, 0:PAIR_ROWS], pair_recv[group, 0:PAIR_ROWS]], axis=0)
        values = jnp.concatenate([pair_send[group, PAIR_ROWS:], pair_recv[group, PAIR_ROWS:]], axis=0)
        values = jnp.concatenate([values, jnp.ones((2 * PAIR_ROWS, LANES), BF16)], axis=1)
        scores = dot_t(queries, keys)
        highest = jnp.max(scores, axis=1, keepdims=True)
        weights = jnp.exp2((scores - highest) * SCALE).astype(BF16)
        upper, lower = split_heads(dot(weights, values), PAIR_ROWS)
        highest = jnp.where(first_lanes, highest[:PAIR_ROWS], highest[PAIR_ROWS:])
        shape = (PAIR_ROWS, 8, LANES)
        result = (upper / lower).reshape(PAIR_ROWS, 1, LANES)
        log = (highest * SCALE + jnp.log2(lower)).reshape(PAIR_ROWS, 1, LANES)
        inside = iota((8, LANES), 0) == lane_offsets(off_pair, group, (8, LANES))
        result = jnp.broadcast_to(result, shape)
        log = jnp.where(inside[None], jnp.broadcast_to(log, shape), LOW)
        own_result = mixed[group].reshape(shape)
        own_log = logs[group].reshape(shape)
        peak = jnp.maximum(own_log, log)
        own_factor = jnp.exp2(own_log - peak)
        factor = jnp.exp2(log - peak)
        both = own_factor + factor
        merged = (own_factor * own_result + factor * result) / both
        log = peak + jnp.log2(both)
        out_ref[:, columns(group)] = merged.reshape(ROWS, LANES).astype(BF16)
        shape = (FAR_ROWS, R_FAR // 8, 8, LANES)
        inside = far_inside(group)
        for place, each in enumerate((merged, log)):
            kept = jnp.where(inside[None], each.reshape(shape), 0.0)
            at_far[group, place] = jnp.sum(jnp.sum(kept, axis=1), axis=1)

    def merge_three(index, carry):
        for inner in range(3):
            pair_copy(index * 3 + inner).wait_recv()
        for inner in range(3):
            merge_pair(index * 3 + inner)
        return carry

    def merge_and_own(index, carry):
        merge_three(index, carry)

        @pl.when(jnp.logical_and(is_owner, index == 0))
        def _():
            own_all()

        return carry

    lax.fori_loop(0, GROUPS // 3, merge_and_own, 0)

    for index in range(len(OWNERS)):
        @pl.when(me != OWNERS[index])
        def _():
            back_copy(index, me).wait_recv()

    is_coarse = lax.rem(iota((1, LANES), 1), HEAD) < HEAD // 2

    def merge_far(group):
        rows = 16 * (group % 2)
        both = back_recv[group // 2, rows : rows + 16].astype(F32)
        result, log = both[:FAR_ROWS], both[FAR_ROWS:]
        log = log + jnp.where(is_coarse, pltpu.roll(log, LANES - HEAD // 2, 1), pltpu.roll(log, HEAD // 2, 1))
        own_result, own_log = at_far[group, 0], at_far[group, 1]
        peak = jnp.maximum(own_log, log)
        own_factor = jnp.exp2(own_log - peak)
        factor = jnp.exp2(log - peak)
        merged = (own_factor * own_result + factor * result) / (own_factor + factor)
        merged = jnp.broadcast_to(merged.reshape(FAR_ROWS, 1, LANES), (FAR_ROWS, 16, LANES)).astype(BF16)
        mask = far_mask(group)
        earlier = out_ref[:, columns(group)].reshape(FAR_ROWS, R_FAR // 16, 16, LANES)
        final = earlier * (jnp.ones((), BF16) - mask)[None] + merged[:, None] * mask[None]
        out_ref[:, columns(group)] = final.reshape(ROWS, LANES)

    for group in range(GROUPS):
        merge_far(group)

    for index in range(len(OWNERS)):
        @pl.when(me != OWNERS[index])
        def _():
            far_copy(index, me).wait_send()

    for group in range(GROUPS):
        pair_copy(group).wait_send()

    @pl.when(is_owner)
    def _():
        for distance in range(1, SHARDS):
            back_copy(0, lax.rem(me + distance, SHARDS)).wait_send()


def local(queries, key_rows, value_rows, offset_two, offset_four, offset_pair, offset_far):
    held = (offset_two, offset_four, offset_pair, offset_far, queries, key_rows, value_rows)
    held = [pltpu.with_memory_space_constraint(each, pltpu.HBM) for each in held]
    anywhere = pl.BlockSpec(memory_space=pltpu.HBM)
    return pl.pallas_call(
        kernel,
        out_shape=jax.ShapeDtypeStruct((ROWS, WIDTH), BF16),
        in_specs=[anywhere] * 7,
        out_specs=pl.BlockSpec(memory_space=pltpu.VMEM),
        scratch_shapes=[
            *[pltpu.SMEM((HEADS,), jnp.int32)] * 4,
            *[pltpu.VMEM((ROWS, WIDTH), BF16)] * 3,
            pltpu.VMEM((GROUPS, 2 * PAIR_ROWS, LANES), BF16),
            pltpu.VMEM((GROUPS, 2 * PAIR_ROWS, LANES), BF16),
            pltpu.VMEM((GROUPS, PAIR_ROWS, LANES), BF16),
            pltpu.VMEM((len(OWNERS), 48, LANES), BF16),
            pltpu.VMEM((SHARDS, 48, LANES), BF16),
            pltpu.VMEM((SHARDS, 32, LANES), BF16),
            pltpu.VMEM((len(OWNERS), 32, LANES), BF16),
            pltpu.VMEM((GROUPS, ROWS, LANES), F32),
            pltpu.VMEM((GROUPS, ROWS, LANES), F32),
            pltpu.VMEM((GROUPS, 2, FAR_ROWS, LANES), F32),
            pltpu.SemaphoreType.DMA((4,)),
            pltpu.SemaphoreType.DMA((3, len(OWNERS))),
            pltpu.SemaphoreType.DMA((GROUPS,)),
            pltpu.SemaphoreType.DMA((GROUPS,)),
            pltpu.SemaphoreType.DMA((len(OWNERS),)),
            pltpu.SemaphoreType.DMA((SHARDS,)),
            pltpu.SemaphoreType.DMA((SHARDS,)),
            pltpu.SemaphoreType.DMA((len(OWNERS),)),
        ],
        compiler_params=pltpu.CompilerParams(
            collective_id=0, has_side_effects=True, vmem_limit_bytes=40 * 1024 * 1024
        ),
        cost_estimate=pl.CostEstimate(flops=2 * 10**9, bytes_accessed=5 * 10**6, transcendentals=6 * 10**6),
        name="dilated_attention",
    )(*held)


def solution(mesh):
    rows = P(("dp", "seq"), None)
    return jax.shard_map(
        local, mesh=mesh, in_specs=(rows,) * 3 + (P(),) * 4, out_specs=rows, check_vma=False
    )
```

```python
import functools
import math

import jax
import jax.numpy as jnp
from jax import lax
from jax.experimental import pallas as pl
from jax.experimental.pallas import tpu as pltpu
from jax.sharding import PartitionSpec as P

R_TWO = 2
R_FOUR = 4
R_PAIR = 8
R_FAR = 64

ROWS = 512
HEADS = 18
HEAD = 64
WIDTH = HEADS * HEAD
GROUPS = HEADS // 2
LANES = 128
SHARDS = 16
PAIR_ROWS = ROWS // R_PAIR
FAR_ROWS = ROWS // R_FAR
SCALE = HEAD**-0.5 * math.log2(math.e)
LOW = -1e30
EARLY = 1
PAIR_OWNER = 1
PAIR_OTHER = 0
OWNERS = (0, 1, 2, 3, 4)
SLAB = 2 * LANES
NEAREST = sorted(range(SHARDS), key=lambda each: min(each, SHARDS - each))

F32 = jnp.float32
BF16 = jnp.bfloat16


def iota(shape, dimension):
    return lax.broadcasted_iota(jnp.int32, shape, dimension)


def dot_t(a, b):
    return lax.dot_general(a, b, (((1,), (1,)), ((), ())), preferred_element_type=F32)


def dot(a, b):
    return lax.dot_general(a, b, (((1,), (0,)), ((), ())), preferred_element_type=F32)


def lane_offsets(ref, group, shape):
    first = iota(shape, len(shape) - 1) < HEAD
    return jnp.where(first, ref[2 * group], ref[2 * group + 1])


def split_heads(result, rows):
    first = iota((1, LANES), 1) < HEAD
    upper = jnp.where(first, result[:rows, :LANES], result[rows:, :LANES])
    lower = jnp.where(first, result[:rows, LANES:], result[rows:, LANES:])
    return upper, lower


def kernel(
    off_two_hbm, off_four_hbm, off_pair_hbm, off_far_hbm, q_hbm, k_hbm, v_hbm, out_ref,
    off_two, off_four, off_pair, off_far, q_ref, k_ref, v_ref,
    pair_send, pair_recv, q_pair, far_send, far_recv, back_send, back_recv, mixed, logs, at_far,
    offset_sems, load_sems, pair_send_sems, pair_recv_sems,
    far_send_sems, far_recv_sems, back_send_sems, back_recv_sems,
):
    me = lax.axis_index("seq")
    partner = me + 1 - 2 * lax.rem(me, 2)
    is_owner, partner_owns = False, False
    mine = 0
    for index, owner in enumerate(OWNERS):
        is_owner = jnp.logical_or(is_owner, me == owner)
        partner_owns = jnp.logical_or(partner_owns, partner == owner)
        mine = jnp.where(me == owner, index, mine)
    group_count = jnp.where(is_owner, jnp.minimum(GROUPS - 2 * mine, 2), 0)
    early = jnp.where(is_owner, EARLY, 0)
    greeted = len(OWNERS) - is_owner.astype(jnp.int32) + 1 - partner_owns.astype(jnp.int32)

    barrier = pltpu.get_barrier_semaphore()

    @pl.when(is_owner)
    def _():
        for distance in range(1, SHARDS):
            pl.semaphore_signal(barrier, inc=1, device_id={"seq": lax.rem(me + distance, SHARDS)})

    @pl.when(jnp.logical_not(is_owner))
    def _():
        pl.semaphore_signal(barrier, inc=1, device_id={"seq": partner})

    offset_loads = [
        pltpu.make_async_copy(source, target, offset_sems.at[index])
        for index, (source, target) in enumerate(
            ((off_far_hbm, off_far), (off_pair_hbm, off_pair), (off_two_hbm, off_two), (off_four_hbm, off_four))
        )
    ]

    def slab_loads(index):
        part = pl.ds(index * SLAB, min(SLAB, WIDTH - index * SLAB))
        return [
            pltpu.make_async_copy(source.at[:, part], target.at[:, part], load_sems.at[which, index])
            for which, (source, target) in enumerate(((q_hbm, q_ref), (k_hbm, k_ref), (v_hbm, v_ref)))
        ]

    for load in offset_loads:
        load.start()
    for index in range(len(OWNERS)):
        for load in slab_loads(index):
            load.start()

    def columns(group):
        start = group * LANES
        return pl.ds(start if isinstance(group, int) else pl.multiple_of(start, LANES), LANES)

    def pair_copy(group):
        return pltpu.make_async_remote_copy(
            src_ref=pair_send.at[group],
            dst_ref=pair_recv.at[group],
            send_sem=pair_send_sems.at[group],
            recv_sem=pair_recv_sems.at[group],
            device_id={"seq": partner},
        )

    def far_copy(index, source):
        rows = pl.ds(0, 48 if 2 * index + 1 < GROUPS else 32)
        return pltpu.make_async_remote_copy(
            src_ref=far_send.at[index, rows],
            dst_ref=far_recv.at[source, rows],
            send_sem=far_send_sems.at[index],
            recv_sem=far_recv_sems.at[source],
            device_id={"seq": OWNERS[index]},
        )

    def back_copy(index, target):
        return pltpu.make_async_remote_copy(
            src_ref=back_send.at[target],
            dst_ref=back_recv.at[index],
            send_sem=back_send_sems.at[target],
            recv_sem=back_recv_sems.at[index],
            device_id={"seq": target},
        )

    first_lanes = iota((1, LANES), 1) < HEAD
    head_lanes = [
        first_lanes.astype(F32).astype(BF16),
        (~first_lanes).astype(F32).astype(BF16),
    ]
    gather_pair = (iota((PAIR_ROWS, ROWS), 1) // R_PAIR == iota((PAIR_ROWS, ROWS), 0)).astype(F32).astype(BF16)
    gather_far = (iota((16, LANES), 1) // 16 == lax.rem(iota((16, LANES), 0), FAR_ROWS)).astype(F32).astype(BF16)

    def far_mask(group):
        shape = (R_FAR // 16, 16, LANES)
        rows = iota(shape, 0) * 16 + iota(shape, 1)
        return (rows == lane_offsets(off_far, group, shape)).astype(F32).astype(BF16)

    def pick_far(source, group, mask):
        shaped = source[:, columns(group)].reshape(FAR_ROWS, R_FAR // 16, 16, LANES) * mask[None]
        picked = (shaped[:, 0] + shaped[:, 1]) + (shaped[:, 2] + shaped[:, 3])
        return dot(gather_far, picked.reshape(FAR_ROWS * 16, LANES))

    def select_far(index):
        low = iota((16, LANES), 0) < FAR_ROWS
        picked = []
        for group in range(2 * index, min(2 * index + 2, GROUPS)):
            mask = far_mask(group)
            picked += [pick_far(source, group, mask) for source in (q_ref, k_ref, v_ref)]
        picked += picked[-1:] * (len(picked) % 2)
        for tile in range(len(picked) // 2):
            both = jnp.where(low, picked[2 * tile], picked[2 * tile + 1])
            far_send[index, 16 * tile : 16 * tile + 16] = both.astype(BF16)

    def pick_pair(source, group, mask):
        shaped = source[:, columns(group)].reshape(ROWS // 16, 16, LANES)
        return dot(gather_pair, (shaped * mask[None]).reshape(ROWS, LANES)).astype(BF16)

    def select_pair(group):
        offsets = lane_offsets(off_pair, group, (16, LANES))
        mask = (lax.rem(iota((16, LANES), 0), R_PAIR) == offsets).astype(F32).astype(BF16)
        pair_send[group, 0:PAIR_ROWS] = pick_pair(k_ref, group, mask)
        pair_send[group, PAIR_ROWS:] = pick_pair(v_ref, group, mask)
        q_pair[group] = pick_pair(q_ref, group, mask)

    def by_threes(work):
        def three(index, carry):
            for inner in range(3):
                work(index * 3 + inner)
            return carry

        lax.fori_loop(0, GROUPS // 3, three, 0)

    def send_far(index):
        @pl.when(me != OWNERS[index])
        def _():
            far_copy(index, me).start()

        @pl.when(me == OWNERS[index])
        def _():
            far_recv[me] = far_send[index]

    @pl.when(early == 0)
    def _():
        pl.semaphore_wait(barrier, greeted)

    for load in offset_loads:
        load.wait()
    for index in range(len(OWNERS)):
        for load in slab_loads(index):
            load.wait()
        select_far(index)

        @pl.when(early == 0)
        def _():
            send_far(index)

    by_threes(select_pair)

    def own(slot):
        parts = []
        for part in range(3):
            place = 3 * slot + part
            start = place // 2 * 16
            tile = far_recv[:, start : start + 16].astype(F32).reshape(SHARDS, 2, FAR_ROWS, LANES)
            parts.append(tile[:, place % 2].reshape(SHARDS * FAR_ROWS, LANES).astype(BF16))
        queries, keys, values = parts
        values = jnp.concatenate([values, jnp.ones((SHARDS * FAR_ROWS, LANES), BF16)], axis=1)
        parts = []
        for parity in range(2):
            scores = dot_t(queries * head_lanes[parity], keys)
            highest = jnp.max(scores, axis=1, keepdims=True)
            weights = jnp.exp2((scores - highest) * SCALE).astype(BF16)
            result = dot(weights, values)
            parts.append((result[:, :LANES], result[:, LANES:], highest))
        upper, lower, highest = (jnp.where(first_lanes, a, b) for a, b in zip(*parts))
        result = (upper / lower).astype(BF16).astype(F32)
        log = highest * SCALE + jnp.log2(lower)
        coarse = log.astype(BF16).astype(F32)
        is_coarse = lax.rem(iota((1, LANES), 1), HEAD) < HEAD // 2
        log = jnp.where(is_coarse, coarse, log - coarse)
        shape = (SHARDS, 1, FAR_ROWS, LANES)
        both = jnp.concatenate([result.reshape(shape), log.reshape(shape)], axis=1)
        return both.reshape(SHARDS, 2 * FAR_ROWS, LANES).astype(BF16)

    def own_all():
        for distance in range(1, SHARDS):
            source = lax.rem(me + distance, SHARDS)

            @pl.when(group_count == 2)
            def _():
                far_copy(0, source).wait_recv()

            @pl.when(group_count == 1)
            def _():
                far_copy(len(OWNERS) - 1, source).wait_recv()

        @pl.when(group_count == 2)
        def _():
            results = [own(0), own(1)]
            for slot, result in enumerate(results):
                back_send[:, 16 * slot : 16 * slot + 16] = result

        @pl.when(group_count == 1)
        def _():
            back_send[:, 0:16] = own(0)

        for target in NEAREST:
            @pl.when(me != target)
            def _():
                back_copy(mine, target).start()

        back_recv[mine] = back_send[me]

    def dense(group):
        queries = q_ref[:, columns(group)]
        keys = k_ref[:, columns(group)]
        values = jnp.concatenate([v_ref[:, columns(group)], jnp.ones((ROWS, LANES), BF16)], axis=1)
        parts = []
        for parity in range(2):
            two = off_two[2 * group + parity]
            four = off_four[2 * group + parity]
            rows, cols = iota((8, LANES), 0), iota((8, LANES), 1)
            in_two = jnp.logical_and(rows % R_TWO == two, cols % R_TWO == two)
            in_four = jnp.logical_and(rows % R_FOUR == four, cols % R_FOUR == four)
            times = 1.0 + in_two.astype(F32) + in_four.astype(F32)
            times = jnp.concatenate([times] * (ROWS // LANES), axis=1)
            scores = dot_t(queries * head_lanes[parity], keys)
            highest = jnp.max(scores, axis=1, keepdims=True)
            raised = jnp.exp2((scores - highest) * SCALE)
            weights = (raised.reshape(ROWS // 8, 8, ROWS) * times[None]).reshape(ROWS, ROWS)
            result = dot(weights.astype(BF16), values)
            parts.append((result[:, :LANES], result[:, LANES:], highest))
        upper, lower, highest = (jnp.where(first_lanes, a, b) for a, b in zip(*parts))
        mixed[group] = upper / lower
        logs[group] = highest * SCALE + jnp.log2(lower)

    def step(group, carry):
        @pl.when(group == early)
        def _():
            @pl.when(early > 0)
            def _():
                pl.semaphore_wait(barrier, greeted)
                for index in range(len(OWNERS)):
                    send_far(index)

        @pl.when(group == jnp.where(is_owner, PAIR_OWNER, PAIR_OTHER))
        def _():
            for chunk in range(GROUPS):
                pair_copy(chunk).start()

        dense(group)
        return carry

    lax.fori_loop(0, GROUPS, step, 0)

    def far_inside(group):
        shape = (R_FAR // 8, 8, LANES)
        return iota(shape, 0) * 8 + iota(shape, 1) == lane_offsets(off_far, group, shape)

    def merge_pair(group):
        queries = q_pair[group]
        queries = jnp.concatenate([queries * head_lanes[0], queries * head_lanes[1]], axis=0)
        keys = jnp.concatenate([pair_send[group, 0:PAIR_ROWS], pair_recv[group, 0:PAIR_ROWS]], axis=0)
        values = jnp.concatenate([pair_send[group, PAIR_ROWS:], pair_recv[group, PAIR_ROWS:]], axis=0)
        values = jnp.concatenate([values, jnp.ones((2 * PAIR_ROWS, LANES), BF16)], axis=1)
        scores = dot_t(queries, keys)
        highest = jnp.max(scores, axis=1, keepdims=True)
        weights = jnp.exp2((scores - highest) * SCALE).astype(BF16)
        upper, lower = split_heads(dot(weights, values), PAIR_ROWS)
        highest = jnp.where(first_lanes, highest[:PAIR_ROWS], highest[PAIR_ROWS:])
        shape = (PAIR_ROWS, 8, LANES)
        result = (upper / lower).reshape(PAIR_ROWS, 1, LANES)
        log = (highest * SCALE + jnp.log2(lower)).reshape(PAIR_ROWS, 1, LANES)
        inside = iota((8, LANES), 0) == lane_offsets(off_pair, group, (8, LANES))
        result = jnp.broadcast_to(result, shape)
        log = jnp.where(inside[None], jnp.broadcast_to(log, shape), LOW)
        own_result = mixed[group].reshape(shape)
        own_log = logs[group].reshape(shape)
        peak = jnp.maximum(own_log, log)
        own_factor = jnp.exp2(own_log - peak)
        factor = jnp.exp2(log - peak)
        both = own_factor + factor
        merged = (own_factor * own_result + factor * result) / both
        log = peak + jnp.log2(both)
        out_ref[:, columns(group)] = merged.reshape(ROWS, LANES).astype(BF16)
        shape = (FAR_ROWS, R_FAR // 8, 8, LANES)
        inside = far_inside(group)
        for place, each in enumerate((merged, log)):
            kept = jnp.where(inside[None], each.reshape(shape), 0.0)
            at_far[group, place] = jnp.sum(jnp.sum(kept, axis=1), axis=1)

    def merge_three(index, carry):
        for inner in range(3):
            pair_copy(index * 3 + inner).wait_recv()
        for inner in range(3):
            merge_pair(index * 3 + inner)
        return carry

    def merge_and_own(index, carry):
        merge_three(index, carry)

        @pl.when(jnp.logical_and(is_owner, index == 0))
        def _():
            own_all()

        return carry

    lax.fori_loop(0, GROUPS // 3, merge_and_own, 0)

    for index in range(len(OWNERS)):
        @pl.when(me != OWNERS[index])
        def _():
            back_copy(index, me).wait_recv()

    is_coarse = lax.rem(iota((1, LANES), 1), HEAD) < HEAD // 2

    def merge_far(group):
        rows = 16 * (group % 2)
        both = back_recv[group // 2, rows : rows + 16].astype(F32)
        result, log = both[:FAR_ROWS], both[FAR_ROWS:]
        log = log + jnp.where(is_coarse, pltpu.roll(log, LANES - HEAD // 2, 1), pltpu.roll(log, HEAD // 2, 1))
        own_result, own_log = at_far[group, 0], at_far[group, 1]
        peak = jnp.maximum(own_log, log)
        own_factor = jnp.exp2(own_log - peak)
        factor = jnp.exp2(log - peak)
        merged = (own_factor * own_result + factor * result) / (own_factor + factor)
        merged = jnp.broadcast_to(merged.reshape(FAR_ROWS, 1, LANES), (FAR_ROWS, 16, LANES)).astype(BF16)
        mask = far_mask(group)
        earlier = out_ref[:, columns(group)].reshape(FAR_ROWS, R_FAR // 16, 16, LANES)
        final = earlier * (jnp.ones((), BF16) - mask)[None] + merged[:, None] * mask[None]
        out_ref[:, columns(group)] = final.reshape(ROWS, LANES)

    for group in range(GROUPS):
        merge_far(group)

    for index in range(len(OWNERS)):
        @pl.when(me != OWNERS[index])
        def _():
            far_copy(index, me).wait_send()

    for group in range(GROUPS):
        pair_copy(group).wait_send()

    @pl.when(is_owner)
    def _():
        for distance in range(1, SHARDS):
            back_copy(0, lax.rem(me + distance, SHARDS)).wait_send()


def local(queries, key_rows, value_rows, offset_two, offset_four, offset_pair, offset_far):
    held = (offset_two, offset_four, offset_pair, offset_far, queries, key_rows, value_rows)
    held = [pltpu.with_memory_space_constraint(each, pltpu.HBM) for each in held]
    anywhere = pl.BlockSpec(memory_space=pltpu.HBM)
    return pl.pallas_call(
        kernel,
        out_shape=jax.ShapeDtypeStruct((ROWS, WIDTH), BF16),
        in_specs=[anywhere] * 7,
        out_specs=pl.BlockSpec(memory_space=pltpu.VMEM),
        scratch_shapes=[
            *[pltpu.SMEM((HEADS,), jnp.int32)] * 4,
            *[pltpu.VMEM((ROWS, WIDTH), BF16)] * 3,
            pltpu.VMEM((GROUPS, 2 * PAIR_ROWS, LANES), BF16),
            pltpu.VMEM((GROUPS, 2 * PAIR_ROWS, LANES), BF16),
            pltpu.VMEM((GROUPS, PAIR_ROWS, LANES), BF16),
            pltpu.VMEM((len(OWNERS), 48, LANES), BF16),
            pltpu.VMEM((SHARDS, 48, LANES), BF16),
            pltpu.VMEM((SHARDS, 32, LANES), BF16),
            pltpu.VMEM((len(OWNERS), 32, LANES), BF16),
            pltpu.VMEM((GROUPS, ROWS, LANES), F32),
            pltpu.VMEM((GROUPS, ROWS, LANES), F32),
            pltpu.VMEM((GROUPS, 2, FAR_ROWS, LANES), F32),
            pltpu.SemaphoreType.DMA((4,)),
            pltpu.SemaphoreType.DMA((3, len(OWNERS))),
            pltpu.SemaphoreType.DMA((GROUPS,)),
            pltpu.SemaphoreType.DMA((GROUPS,)),
            pltpu.SemaphoreType.DMA((len(OWNERS),)),
            pltpu.SemaphoreType.DMA((SHARDS,)),
            pltpu.SemaphoreType.DMA((SHARDS,)),
            pltpu.SemaphoreType.DMA((len(OWNERS),)),
        ],
        compiler_params=pltpu.CompilerParams(
            collective_id=0, has_side_effects=True, vmem_limit_bytes=40 * 1024 * 1024
        ),
        cost_estimate=pl.CostEstimate(flops=2 * 10**9, bytes_accessed=5 * 10**6, transcendentals=6 * 10**6),
        name="dilated_attention",
    )(*held)


def solution(mesh):
    rows = P(("dp", "seq"), None)
    return jax.shard_map(
        local, mesh=mesh, in_specs=(rows,) * 3 + (P(),) * 4, out_specs=rows, check_vma=False
    )
```

```python
import functools
import math

import jax
import jax.numpy as jnp
from jax import lax
from jax.experimental import pallas as pl
from jax.experimental.pallas import tpu as pltpu
from jax.sharding import PartitionSpec as P

R_TWO = 2
R_FOUR = 4
R_PAIR = 8
R_FAR = 64

ROWS = 512
HEADS = 18
HEAD = 64
WIDTH = HEADS * HEAD
GROUPS = HEADS // 2
LANES = 128
SHARDS = 16
PAIR_ROWS = ROWS // R_PAIR
FAR_ROWS = ROWS // R_FAR
SCALE = HEAD**-0.5 * math.log2(math.e)
LOW = -1e30
EARLY = 1
PAIR_OWNER = 1
PAIR_OTHER = 0
OWNERS = (0, 1, 2, 3, 4)
SLAB = 2 * LANES
NEAREST = sorted(range(SHARDS), key=lambda each: min(each, SHARDS - each))

F32 = jnp.float32
BF16 = jnp.bfloat16


def iota(shape, dimension):
    return lax.broadcasted_iota(jnp.int32, shape, dimension)


def dot_t(a, b):
    return lax.dot_general(a, b, (((1,), (1,)), ((), ())), preferred_element_type=F32)


def dot(a, b):
    return lax.dot_general(a, b, (((1,), (0,)), ((), ())), preferred_element_type=F32)


def lane_offsets(ref, group, shape):
    first = iota(shape, len(shape) - 1) < HEAD
    return jnp.where(first, ref[2 * group], ref[2 * group + 1])


def split_heads(result, rows):
    first = iota((1, LANES), 1) < HEAD
    upper = jnp.where(first, result[:rows, :LANES], result[rows:, :LANES])
    lower = jnp.where(first, result[:rows, LANES:], result[rows:, LANES:])
    return upper, lower


def kernel(
    off_two_hbm, off_four_hbm, off_pair_hbm, off_far_hbm, q_hbm, k_hbm, v_hbm, out_ref,
    off_two, off_four, off_pair, off_far, q_ref, k_ref, v_ref,
    pair_send, pair_recv, q_pair, far_send, far_recv, back_send, back_recv, mixed, logs, at_far,
    offset_sems, load_sems, pair_send_sems, pair_recv_sems,
    far_send_sems, far_recv_sems, back_send_sems, back_recv_sems,
):
    me = lax.axis_index("seq")
    partner = me + 1 - 2 * lax.rem(me, 2)
    is_owner, partner_owns = False, False
    mine = 0
    for index, owner in enumerate(OWNERS):
        is_owner = jnp.logical_or(is_owner, me == owner)
        partner_owns = jnp.logical_or(partner_owns, partner == owner)
        mine = jnp.where(me == owner, index, mine)
    group_count = jnp.where(is_owner, jnp.minimum(GROUPS - 2 * mine, 2), 0)
    early = jnp.where(is_owner, EARLY, 0)
    greeted = len(OWNERS) - is_owner.astype(jnp.int32) + 1 - partner_owns.astype(jnp.int32)

    barrier = pltpu.get_barrier_semaphore()

    @pl.when(is_owner)
    def _():
        for distance in range(1, SHARDS):
            pl.semaphore_signal(barrier, inc=1, device_id={"seq": lax.rem(me + distance, SHARDS)})

    @pl.when(jnp.logical_not(is_owner))
    def _():
        pl.semaphore_signal(barrier, inc=1, device_id={"seq": partner})

    offset_loads = [
        pltpu.make_async_copy(source, target, offset_sems.at[index])
        for index, (source, target) in enumerate(
            ((off_far_hbm, off_far), (off_pair_hbm, off_pair), (off_two_hbm, off_two), (off_four_hbm, off_four))
        )
    ]

    def slab_loads(index):
        part = pl.ds(index * SLAB, min(SLAB, WIDTH - index * SLAB))
        return [
            pltpu.make_async_copy(source.at[:, part], target.at[:, part], load_sems.at[which, index])
            for which, (source, target) in enumerate(((q_hbm, q_ref), (k_hbm, k_ref), (v_hbm, v_ref)))
        ]

    for load in offset_loads:
        load.start()
    for index in range(len(OWNERS)):
        for load in slab_loads(index):
            load.start()

    def columns(group):
        start = group * LANES
        return pl.ds(start if isinstance(group, int) else pl.multiple_of(start, LANES), LANES)

    def pair_copy(group):
        return pltpu.make_async_remote_copy(
            src_ref=pair_send.at[group],
            dst_ref=pair_recv.at[group],
            send_sem=pair_send_sems.at[group],
            recv_sem=pair_recv_sems.at[group],
            device_id={"seq": partner},
        )

    def far_copy(index, source):
        rows = pl.ds(0, 48 if 2 * index + 1 < GROUPS else 32)
        return pltpu.make_async_remote_copy(
            src_ref=far_send.at[index, rows],
            dst_ref=far_recv.at[source, rows],
            send_sem=far_send_sems.at[index],
            recv_sem=far_recv_sems.at[source],
            device_id={"seq": OWNERS[index]},
        )

    def back_copy(index, target):
        return pltpu.make_async_remote_copy(
            src_ref=back_send.at[target],
            dst_ref=back_recv.at[index],
            send_sem=back_send_sems.at[target],
            recv_sem=back_recv_sems.at[index],
            device_id={"seq": target},
        )

    first_lanes = iota((1, LANES), 1) < HEAD
    head_lanes = [
        first_lanes.astype(F32).astype(BF16),
        (~first_lanes).astype(F32).astype(BF16),
    ]
    gather_pair = (iota((PAIR_ROWS, ROWS), 1) // R_PAIR == iota((PAIR_ROWS, ROWS), 0)).astype(F32).astype(BF16)
    gather_far = (iota((16, LANES), 1) // 16 == lax.rem(iota((16, LANES), 0), FAR_ROWS)).astype(F32).astype(BF16)

    def far_mask(group):
        shape = (R_FAR // 16, 16, LANES)
        rows = iota(shape, 0) * 16 + iota(shape, 1)
        return (rows == lane_offsets(off_far, group, shape)).astype(F32).astype(BF16)

    def pick_far(source, group, mask):
        shaped = source[:, columns(group)].reshape(FAR_ROWS, R_FAR // 16, 16, LANES) * mask[None]
        picked = (shaped[:, 0] + shaped[:, 1]) + (shaped[:, 2] + shaped[:, 3])
        return dot(gather_far, picked.reshape(FAR_ROWS * 16, LANES))

    def select_far(index):
        low = iota((16, LANES), 0) < FAR_ROWS
        picked = []
        for group in range(2 * index, min(2 * index + 2, GROUPS)):
            mask = far_mask(group)
            picked += [pick_far(source, group, mask) for source in (q_ref, k_ref, v_ref)]
        picked += picked[-1:] * (len(picked) % 2)
        for tile in range(len(picked) // 2):
            both = jnp.where(low, picked[2 * tile], picked[2 * tile + 1])
            far_send[index, 16 * tile : 16 * tile + 16] = both.astype(BF16)

    def pick_pair(source, group, mask):
        shaped = source[:, columns(group)].reshape(ROWS // 16, 16, LANES)
        return dot(gather_pair, (shaped * mask[None]).reshape(ROWS, LANES)).astype(BF16)

    def select_pair(group):
        offsets = lane_offsets(off_pair, group, (16, LANES))
        mask = (lax.rem(iota((16, LANES), 0), R_PAIR) == offsets).astype(F32).astype(BF16)
        pair_send[group, 0:PAIR_ROWS] = pick_pair(k_ref, group, mask)
        pair_send[group, PAIR_ROWS:] = pick_pair(v_ref, group, mask)
        q_pair[group] = pick_pair(q_ref, group, mask)

    def by_threes(work):
        def three(index, carry):
            for inner in range(3):
                work(index * 3 + inner)
            return carry

        lax.fori_loop(0, GROUPS // 3, three, 0)

    def send_far(index):
        @pl.when(me != OWNERS[index])
        def _():
            far_copy(index, me).start()

        @pl.when(me == OWNERS[index])
        def _():
            far_recv[me] = far_send[index]

    @pl.when(early == 0)
    def _():
        pl.semaphore_wait(barrier, greeted)

    for load in offset_loads:
        load.wait()
    for index in range(len(OWNERS)):
        for load in slab_loads(index):
            load.wait()
        select_far(index)

        @pl.when(early == 0)
        def _():
            send_far(index)

    by_threes(select_pair)

    def own(slot):
        parts = []
        for part in range(3):
            place = 3 * slot + part
            start = place // 2 * 16
            tile = far_recv[:, start : start + 16].astype(F32).reshape(SHARDS, 2, FAR_ROWS, LANES)
            parts.append(tile[:, place % 2].reshape(SHARDS * FAR_ROWS, LANES).astype(BF16))
        queries, keys, values = parts
        values = jnp.concatenate([values, jnp.ones((SHARDS * FAR_ROWS, LANES), BF16)], axis=1)
        parts = []
        for parity in range(2):
            scores = dot_t(queries * head_lanes[parity], keys)
            highest = jnp.max(scores, axis=1, keepdims=True)
            weights = jnp.exp2((scores - highest) * SCALE).astype(BF16)
            result = dot(weights, values)
            parts.append((result[:, :LANES], result[:, LANES:], highest))
        upper, lower, highest = (jnp.where(first_lanes, a, b) for a, b in zip(*parts))
        result = (upper / lower).astype(BF16).astype(F32)
        log = highest * SCALE + jnp.log2(lower)
        coarse = log.astype(BF16).astype(F32)
        is_coarse = lax.rem(iota((1, LANES), 1), HEAD) < HEAD // 2
        log = jnp.where(is_coarse, coarse, log - coarse)
        shape = (SHARDS, 1, FAR_ROWS, LANES)
        both = jnp.concatenate([result.reshape(shape), log.reshape(shape)], axis=1)
        return both.reshape(SHARDS, 2 * FAR_ROWS, LANES).astype(BF16)

    def own_all():
        for distance in range(1, SHARDS):
            source = lax.rem(me + distance, SHARDS)

            @pl.when(group_count == 2)
            def _():
                far_copy(0, source).wait_recv()

            @pl.when(group_count == 1)
            def _():
                far_copy(len(OWNERS) - 1, source).wait_recv()

        @pl.when(group_count == 2)
        def _():
            results = [own(0), own(1)]
            for slot, result in enumerate(results):
                back_send[:, 16 * slot : 16 * slot + 16] = result

        @pl.when(group_count == 1)
        def _():
            back_send[:, 0:16] = own(0)

        for target in NEAREST:
            @pl.when(me != target)
            def _():
                back_copy(mine, target).start()

        back_recv[mine] = back_send[me]

    def dense(group):
        queries = q_ref[:, columns(group)]
        keys = k_ref[:, columns(group)]
        values = jnp.concatenate([v_ref[:, columns(group)], jnp.ones((ROWS, LANES), BF16)], axis=1)
        parts = []
        for parity in range(2):
            two = off_two[2 * group + parity]
            four = off_four[2 * group + parity]
            rows, cols = iota((8, LANES), 0), iota((8, LANES), 1)
            in_two = jnp.logical_and(rows % R_TWO == two, cols % R_TWO == two)
            in_four = jnp.logical_and(rows % R_FOUR == four, cols % R_FOUR == four)
            times = 1.0 + in_two.astype(F32) + in_four.astype(F32)
            times = jnp.concatenate([times] * (ROWS // LANES), axis=1)
            scores = dot_t(queries * head_lanes[parity], keys)
            highest = jnp.max(scores, axis=1, keepdims=True)
            raised = jnp.exp2((scores - highest) * SCALE)
            weights = (raised.reshape(ROWS // 8, 8, ROWS) * times[None]).reshape(ROWS, ROWS)
            result = dot(weights.astype(BF16), values)
            parts.append((result[:, :LANES], result[:, LANES:], highest))
        upper, lower, highest = (jnp.where(first_lanes, a, b) for a, b in zip(*parts))
        mixed[group] = upper / lower
        logs[group] = highest * SCALE + jnp.log2(lower)

    def step(group, carry):
        @pl.when(group == early)
        def _():
            @pl.when(early > 0)
            def _():
                pl.semaphore_wait(barrier, greeted)
                for index in range(len(OWNERS)):
                    send_far(index)

        @pl.when(group == jnp.where(is_owner, PAIR_OWNER, PAIR_OTHER))
        def _():
            for chunk in range(GROUPS):
                pair_copy(chunk).start()

        dense(group)
        return carry

    lax.fori_loop(0, GROUPS, step, 0)

    def far_inside(group):
        shape = (R_FAR // 8, 8, LANES)
        return iota(shape, 0) * 8 + iota(shape, 1) == lane_offsets(off_far, group, shape)

    def merge_pair(group):
        queries = q_pair[group]
        queries = jnp.concatenate([queries * head_lanes[0], queries * head_lanes[1]], axis=0)
        keys = jnp.concatenate([pair_send[group, 0:PAIR_ROWS], pair_recv[group, 0:PAIR_ROWS]], axis=0)
        values = jnp.concatenate([pair_send[group, PAIR_ROWS:], pair_recv[group, PAIR_ROWS:]], axis=0)
        values = jnp.concatenate([values, jnp.ones((2 * PAIR_ROWS, LANES), BF16)], axis=1)
        scores = dot_t(queries, keys)
        highest = jnp.max(scores, axis=1, keepdims=True)
        weights = jnp.exp2((scores - highest) * SCALE).astype(BF16)
        upper, lower = split_heads(dot(weights, values), PAIR_ROWS)
        highest = jnp.where(first_lanes, highest[:PAIR_ROWS], highest[PAIR_ROWS:])
        shape = (PAIR_ROWS, 8, LANES)
        result = (upper / lower).reshape(PAIR_ROWS, 1, LANES)
        log = (highest * SCALE + jnp.log2(lower)).reshape(PAIR_ROWS, 1, LANES)
        inside = iota((8, LANES), 0) == lane_offsets(off_pair, group, (8, LANES))
        result = jnp.broadcast_to(result, shape)
        log = jnp.where(inside[None], jnp.broadcast_to(log, shape), LOW)
        own_result = mixed[group].reshape(shape)
        own_log = logs[group].reshape(shape)
        peak = jnp.maximum(own_log, log)
        own_factor = jnp.exp2(own_log - peak)
        factor = jnp.exp2(log - peak)
        both = own_factor + factor
        merged = (own_factor * own_result + factor * result) / both
        log = peak + jnp.log2(both)
        out_ref[:, columns(group)] = merged.reshape(ROWS, LANES).astype(BF16)
        shape = (FAR_ROWS, R_FAR // 8, 8, LANES)
        inside = far_inside(group)
        for place, each in enumerate((merged, log)):
            kept = jnp.where(inside[None], each.reshape(shape), 0.0)
            at_far[group, place] = jnp.sum(jnp.sum(kept, axis=1), axis=1)

    def merge_three(index, carry):
        for inner in range(3):
            pair_copy(index * 3 + inner).wait_recv()
        for inner in range(3):
            merge_pair(index * 3 + inner)
        return carry

    def merge_and_own(index, carry):
        merge_three(index, carry)

        @pl.when(jnp.logical_and(is_owner, index == 0))
        def _():
            own_all()

        return carry

    lax.fori_loop(0, GROUPS // 3, merge_and_own, 0)

    is_coarse = lax.rem(iota((1, LANES), 1), HEAD) < HEAD // 2

    def merge_far(group):
        rows = 16 * (group % 2)
        both = back_recv[group // 2, rows : rows + 16].astype(F32)
        result, log = both[:FAR_ROWS], both[FAR_ROWS:]
        log = log + jnp.where(is_coarse, pltpu.roll(log, LANES - HEAD // 2, 1), pltpu.roll(log, HEAD // 2, 1))
        own_result, own_log = at_far[group, 0], at_far[group, 1]
        peak = jnp.maximum(own_log, log)
        own_factor = jnp.exp2(own_log - peak)
        factor = jnp.exp2(log - peak)
        merged = (own_factor * own_result + factor * result) / (own_factor + factor)
        merged = jnp.broadcast_to(merged.reshape(FAR_ROWS, 1, LANES), (FAR_ROWS, 16, LANES)).astype(BF16)
        mask = far_mask(group)
        earlier = out_ref[:, columns(group)].reshape(FAR_ROWS, R_FAR // 16, 16, LANES)
        final = earlier * (jnp.ones((), BF16) - mask)[None] + merged[:, None] * mask[None]
        out_ref[:, columns(group)] = final.reshape(ROWS, LANES)

    for index in range(len(OWNERS)):
        @pl.when(me != OWNERS[index])
        def _():
            back_copy(index, me).wait_recv()

        for group in range(2 * index, min(2 * index + 2, GROUPS)):
            merge_far(group)

    for index in range(len(OWNERS)):
        @pl.when(me != OWNERS[index])
        def _():
            far_copy(index, me).wait_send()

    for group in range(GROUPS):
        pair_copy(group).wait_send()

    @pl.when(is_owner)
    def _():
        for distance in range(1, SHARDS):
            back_copy(0, lax.rem(me + distance, SHARDS)).wait_send()


def local(queries, key_rows, value_rows, offset_two, offset_four, offset_pair, offset_far):
    held = (offset_two, offset_four, offset_pair, offset_far, queries, key_rows, value_rows)
    held = [pltpu.with_memory_space_constraint(each, pltpu.HBM) for each in held]
    anywhere = pl.BlockSpec(memory_space=pltpu.HBM)
    return pl.pallas_call(
        kernel,
        out_shape=jax.ShapeDtypeStruct((ROWS, WIDTH), BF16),
        in_specs=[anywhere] * 7,
        out_specs=pl.BlockSpec(memory_space=pltpu.VMEM),
        scratch_shapes=[
            *[pltpu.SMEM((HEADS,), jnp.int32)] * 4,
            *[pltpu.VMEM((ROWS, WIDTH), BF16)] * 3,
            pltpu.VMEM((GROUPS, 2 * PAIR_ROWS, LANES), BF16),
            pltpu.VMEM((GROUPS, 2 * PAIR_ROWS, LANES), BF16),
            pltpu.VMEM((GROUPS, PAIR_ROWS, LANES), BF16),
            pltpu.VMEM((len(OWNERS), 48, LANES), BF16),
            pltpu.VMEM((SHARDS, 48, LANES), BF16),
            pltpu.VMEM((SHARDS, 32, LANES), BF16),
            pltpu.VMEM((len(OWNERS), 32, LANES), BF16),
            pltpu.VMEM((GROUPS, ROWS, LANES), F32),
            pltpu.VMEM((GROUPS, ROWS, LANES), F32),
            pltpu.VMEM((GROUPS, 2, FAR_ROWS, LANES), F32),
            pltpu.SemaphoreType.DMA((4,)),
            pltpu.SemaphoreType.DMA((3, len(OWNERS))),
            pltpu.SemaphoreType.DMA((GROUPS,)),
            pltpu.SemaphoreType.DMA((GROUPS,)),
            pltpu.SemaphoreType.DMA((len(OWNERS),)),
            pltpu.SemaphoreType.DMA((SHARDS,)),
            pltpu.SemaphoreType.DMA((SHARDS,)),
            pltpu.SemaphoreType.DMA((len(OWNERS),)),
        ],
        compiler_params=pltpu.CompilerParams(
            collective_id=0, has_side_effects=True, vmem_limit_bytes=40 * 1024 * 1024
        ),
        cost_estimate=pl.CostEstimate(flops=2 * 10**9, bytes_accessed=5 * 10**6, transcendentals=6 * 10**6),
        name="dilated_attention",
    )(*held)


def solution(mesh):
    rows = P(("dp", "seq"), None)
    return jax.shard_map(
        local, mesh=mesh, in_specs=(rows,) * 3 + (P(),) * 4, out_specs=rows, check_vma=False
    )
```
